256 devices in a mesh: seg: 16 (over y, x), sec: 16 (over z, core).
Axes of the slice: x: 4, y: 4, z: 8, core: 2. Of those that a mesh axis runs over, the one named last changes fastest.
Arguments:
- psi: bfloat16 [16, 16, 16, 128, 128], P('seg', 'sec'), may hold values from -6 to 6
- env_build: bfloat16 [16, 16, 12, 128, 128], P('seg', 'sec'), may hold values from -0.5 to 0.5
- env_right: bfloat16 [16, 16, 12, 128, 128], P('seg', 'sec'), may hold values from -0.5 to 0.5
- site_left: bfloat16 [12, 12, 4, 4], replicated, may hold values from -0.4375 to 0.4375
- site_right: bfloat16 [12, 12, 4, 4], replicated, may hold values from -0.4375 to 0.4375
- charge: int32 [16], replicated, may hold values from 0 to 15
- rank: int32 [16], P('sec'), may hold values from 64 to 128
Outputs:
- state: bfloat16 [16, 16, 16, 128, 128], P('seg', 'sec')
- energy: float32 [16], P('seg')
- sector_weight: float32 [16, 16], P('seg', 'sec')
The draws below stay inside these ranges and needn't reach their ends.
All inputs are finite; a program needn't handle non-finite values.
Results may differ from the reference program's by a relative error of at most 0.012.
Values may be sent and summed in bfloat16 or wider, within the bound.
No kernel may reach another device: no remote copies, remote signals or barrier semaphores. Data moves between devices by JAX's collectives and lax.ppermute only.
A program may use at most 128 MiB of HBM per device.

```python
import jax
import jax.numpy as jnp
from jax import lax

B = 128
W = 12
D = 4
ITERS = 2
P_SIZE = 16
SECTORS = 16
SEGS = 16


def with_ends(values, rng, low, top_value):
    longest = values.shape.index(max(values.shape))
    spots = []
    for shift in (0, 1):
        where = [jax.random.randint(jax.random.fold_in(rng, axis), (), 0, length) for axis, length in enumerate(values.shape)]
        where[longest] = (where[longest] + shift) % values.shape[longest]
        spots.append(tuple(where))
    return values.at[spots[0]].set(low).at[spots[1]].set(top_value)


def block_scale(own_key, shape, cuts, low, top_value):
    gain = 1.0
    for axis_at, shards_of in cuts:
        heights = jax.random.uniform(jax.random.fold_in(jax.random.fold_in(own_key, 6), axis_at), (shards_of,), jnp.float32, low / len(cuts), top_value / len(cuts))
        gain = gain * jnp.repeat(jnp.exp(heights), shape[axis_at] // shards_of).reshape((-1,) + (1,) * (len(shape) - 1 - axis_at))
    return gain


def bell_draw(own_key, dims, deviation, most, shards=(), dtype=jnp.bfloat16):
    factor_of = block_scale(own_key, dims, shards, -0.22, 0.18) if shards else 1.0
    array = jax.random.normal(own_key, dims, jnp.float32) * deviation * factor_of
    return jnp.minimum(jnp.maximum(array, -most), most).astype(dtype)


def setup_inputs(seed: int = 0) -> dict:
    seeds = jax.random.split(jax.random.key(seed), 8)
    psi = bell_draw(seeds[0], (SEGS, SECTORS, P_SIZE, B, B), 1.0, 6.0, ((0, 16), (1, 16)))
    env_build = bell_draw(seeds[1], (SEGS, SECTORS, W, B, B), B ** -0.5, 0.5, ((0, 16), (1, 16)))
    env_right = bell_draw(seeds[2], (SEGS, SECTORS, W, B, B), B ** -0.5, 0.5, ((0, 16), (1, 16)))
    site_left = bell_draw(seeds[3], (W, W, D, D), (W * D * D) ** -0.5, 0.4375)
    site_right = bell_draw(seeds[4], (W, W, D, D), (W * D * D) ** -0.5, 0.4375)
    charge = with_ends(jax.random.randint(seeds[5], (P_SIZE,), 0, SECTORS), jax.random.fold_in(seeds[5], 1), 0, SECTORS - 1).astype(jnp.int32)
    rank = with_ends(jax.random.randint(seeds[6], (SECTORS,), B // 2, B + 1), jax.random.fold_in(seeds[6], 1), B // 2, B).astype(jnp.int32)
    return {"psi": psi, "env_build": env_build, "env_right": env_right, "site_left": site_left, "site_right": site_right, "charge": charge, "rank": rank}


def pair_mpo(site_left, site_right):
    joined = jnp.einsum('lmxs,mwyt->lwxyst', site_left.astype(jnp.float32), site_right.astype(jnp.float32))
    width = joined.shape[0]
    local = joined.shape[2]
    return joined.reshape(width, width, local * local, local * local).astype(jnp.bfloat16)

def apply_block(x_sector, lenv, renv, mpo, left_row):
    first = jnp.einsum('pab,wbc->pwac', x_sector.astype(jnp.float32), renv.astype(jnp.float32)).astype(jnp.bfloat16)
    third = jnp.einsum('lwqp,pwac->lqac', mpo.astype(jnp.float32), first.astype(jnp.float32)).astype(jnp.bfloat16)
    chosen = jnp.take(lenv, left_row, axis=0)
    return jnp.einsum('qlxa,lqac->qxc', chosen.astype(jnp.float32), third.astype(jnp.float32))

def reference(psi, env_build, env_right, site_left, site_right, charge, rank):
    mpo = pair_mpo(site_left, site_right)
    sectors = psi.shape[1]
    left_of = ((jnp.arange(sectors).astype(jnp.int32)[:, None] - charge[None, :]) % sectors).astype(jnp.int32)
    columns = jnp.arange(B).astype(jnp.int32)
    keep = (columns[None, :] < rank[:, None])[:, None, None, :]
    lin = jnp.concatenate([env_build[:1], env_build[:-1]], axis=0)
    count = float(sectors * P_SIZE * B * B)

    def segment(items):
        psi_seg, lenv, renv = items
        x = psi_seg
        energy = jnp.zeros((), jnp.float32)
        squares = jnp.ones((sectors,), jnp.float32)
        total = jnp.ones((), jnp.float32)
        for step in range(ITERS):
            h = jax.vmap(apply_block, in_axes=(0, None, 0, None, 0))(x, lenv, renv, mpo, left_of)
            xf = x.astype(jnp.float32)
            u = jnp.where(keep, xf - 0.5 * h, 0.0)
            squares = lax.optimization_barrier(jnp.sum(u * u, axis=(1, 2, 3)))
            total = jnp.sum(squares)
            energy = jnp.sum(xf * h) / jnp.sum(xf * xf)
            x = (u * lax.rsqrt(total / count + 1e-06)).astype(jnp.bfloat16)
        return (x, energy, jnp.log(float(sectors) * squares / total))
    state, energy, shares = lax.map(segment, (psi, lin, env_right))
    weight = jnp.cumsum(shares, axis=0)
    return (state, energy, weight)
```

```python
import functools

import jax
import jax.numpy as jnp
from jax import lax
from jax.experimental import pallas as pl
from jax.experimental.pallas import tpu as pltpu
from jax.sharding import PartitionSpec as P

F32 = jnp.float32
BF16 = jnp.bfloat16
VMEM_LIMIT = 48 * 2**20


def pair_mpo(site_left, site_right):
    joined = jnp.einsum("lmxs,mwyt->lxywst", site_left, site_right, preferred_element_type=F32)
    rows = joined.shape[0] * joined.shape[1] * joined.shape[2]
    return joined.reshape(rows, rows).astype(BF16)


def spread(xt_ref, renv_ref, mpo_ref, x3_ref):
    states = xt_ref.shape[0]
    pairs = xt_ref.shape[1]
    width = renv_ref.shape[2]
    bonds = renv_ref.shape[0]
    mpo = mpo_ref[...]

    def chunk(j, carry):
        at = pl.multiple_of(j * 16, 16)
        xa = xt_ref[pl.ds(at, 16)].reshape(16 * pairs, width)
        first = []
        for k in range(bonds // 2):
            both = jnp.concatenate([renv_ref[2 * k], renv_ref[2 * k + 1]], axis=1)
            got = jnp.dot(xa, both, preferred_element_type=F32).astype(BF16)
            first.append(got[:, :width])
            first.append(got[:, width:])
        rows = []
        for i in range(8):
            sides = []
            for a in (2 * i, 2 * i + 1):
                sides.append(jnp.concatenate([f[a * pairs : (a + 1) * pairs] for f in first], axis=0))
            rhs = jnp.concatenate(sides, axis=1)
            out = jnp.dot(mpo, rhs, preferred_element_type=F32).astype(BF16)
            rows.append(out[:, :width])
            rows.append(out[:, width:])
        for l in range(bonds):
            block = jnp.stack([row[l * pairs : (l + 1) * pairs] for row in rows], axis=0)
            x3_ref[:, l, pl.ds(at, 16), :] = jnp.swapaxes(block, 0, 1)
        return carry

    lax.fori_loop(0, states // 16, chunk, 0)


def front_kernel(psi_ref, renv_ref, mpo_ref, x3_ref, xt_ref):
    for j in range(psi_ref.shape[1] // 16):
        xt_ref[j * 16 : (j + 1) * 16] = jnp.swapaxes(psi_ref[:, j * 16 : (j + 1) * 16, :], 0, 1)
    spread(xt_ref, renv_ref, mpo_ref, x3_ref)


def contract(lenv_ref, slot, x3_ref, q):
    bonds = lenv_ref.shape[1]
    total = None
    for k in range(bonds // 2):
        lhs = jnp.concatenate([lenv_ref[slot, 2 * k], lenv_ref[slot, 2 * k + 1]], axis=1)
        rhs = jnp.concatenate([x3_ref[q, 2 * k], x3_ref[q, 2 * k + 1]], axis=0)
        part = jnp.dot(lhs, rhs, preferred_element_type=F32)
        total = part if total is None else total + part
    return total


def back_kernel(slot_ref, rank_ref, psi_ref, renv_ref, mpo_ref, x3in_ref, *rest):
    blocks = rest[:16]
    v_ref, stat_ref, lenv_ref, x3_ref, u_ref, xt_ref, sem_ref, sem3_ref = rest[16:]
    pairs, width = psi_ref.shape[0], psi_ref.shape[2]
    copies = [pltpu.make_async_copy(blocks[i], lenv_ref.at[i], sem_ref.at[i]) for i in range(16)]
    for copy in copies:
        copy.start()
    copy3 = pltpu.make_async_copy(x3in_ref, x3_ref, sem3_ref)
    copy3.start()
    keep = lax.broadcasted_iota(jnp.int32, (width, width), 1) < rank_ref[0]
    for copy in copies:
        copy.wait()
    copy3.wait()

    def one(q, acc):
        h = contract(lenv_ref, slot_ref[q], x3_ref, q)
        u = jnp.where(keep, psi_ref[q].astype(F32) - 0.5 * h, 0.0)
        u_ref[q] = u.astype(BF16)
        return acc + u * u

    zero = jnp.zeros((width, width), F32)
    first_sq = lax.fori_loop(0, pairs, one, zero)
    for j in range(width // 16):
        xt_ref[j * 16 : (j + 1) * 16] = jnp.swapaxes(u_ref[:, j * 16 : (j + 1) * 16, :], 0, 1)
    spread(xt_ref, renv_ref, mpo_ref, x3_ref)

    def two(q, accs):
        sq, inner, own = accs
        h = contract(lenv_ref, slot_ref[q], x3_ref, q)
        x = u_ref[q].astype(F32)
        v = jnp.where(keep, x - 0.5 * h, 0.0)
        v_ref[q] = v
        return sq + v * v, inner + x * h, own + x * x

    sq, inner, own = lax.fori_loop(0, pairs, two, (zero, zero, zero))
    row = lax.broadcasted_iota(jnp.int32, (8, width), 0)
    stat = jnp.zeros((8, width), F32)
    for i, part in enumerate((first_sq, sq, inner, own)):
        stat = jnp.where(row == i, jnp.sum(part), stat)
    stat_ref[...] = stat


def front(psi, renv, mpo):
    pairs, width = psi.shape[0], psi.shape[2]
    bonds = renv.shape[0]
    return pl.pallas_call(
        front_kernel,
        out_shape=jax.ShapeDtypeStruct((pairs, bonds, width, width), BF16),
        in_specs=[pl.BlockSpec(memory_space=pltpu.VMEM)] * 3,
        out_specs=pl.BlockSpec(memory_space=pltpu.VMEM),
        scratch_shapes=[pltpu.VMEM((width, pairs, width), BF16)],
        compiler_params=pltpu.CompilerParams(vmem_limit_bytes=VMEM_LIMIT),
        cost_estimate=pl.CostEstimate(flops=2 * 10**9, bytes_accessed=8 * 10**6, transcendentals=0),
        name="front",
    )(psi, renv, mpo)


def back(slot, rank, psi, renv, mpo, x3, blocks):
    pairs, width = psi.shape[0], psi.shape[2]
    bonds = renv.shape[0]
    vmem = pl.BlockSpec(memory_space=pltpu.VMEM)
    smem = pl.BlockSpec(memory_space=pltpu.SMEM)
    anywhere = pl.BlockSpec(memory_space=pl.ANY)
    return pl.pallas_call(
        back_kernel,
        out_shape=(
            jax.ShapeDtypeStruct((pairs, width, width), F32),
            jax.ShapeDtypeStruct((8, width), F32),
        ),
        in_specs=[smem, smem, vmem, vmem, vmem, anywhere] + [anywhere] * 16,
        out_specs=(vmem, vmem),
        scratch_shapes=[
            pltpu.VMEM((16, bonds, width, width), BF16),
            pltpu.VMEM((pairs, bonds, width, width), BF16),
            pltpu.VMEM((pairs, width, width), BF16),
            pltpu.VMEM((width, pairs, width), BF16),
            pltpu.SemaphoreType.DMA((16,)),
            pltpu.SemaphoreType.DMA,
        ],
        compiler_params=pltpu.CompilerParams(vmem_limit_bytes=VMEM_LIMIT),
        cost_estimate=pl.CostEstimate(flops=4 * 10**9, bytes_accessed=16 * 10**6, transcendentals=0),
        name="back",
    )(slot, rank, psi, renv, mpo, x3, *blocks)


def hop(value):
    n = lax.axis_size("sec")
    return lax.ppermute(value, "sec", [(i, (i + (2 if i % 2 == 0 else -2)) % n) for i in range(n)])


def twin(value):
    n = lax.axis_size("sec")
    return lax.ppermute(value, "sec", [(i, i ^ 1) for i in range(n)])


def from_behind(value):
    n = lax.axis_size("seg")
    return lax.ppermute(value, "seg", [(i, i + 1) for i in range(n - 1)])


def shards(psi, env_build, env_right, site_left, site_right, charge, rank):
    nsec = lax.axis_size("sec")
    nseg = lax.axis_size("seg")
    sector = lax.axis_index("sec")
    segment = lax.axis_index("seg")
    x = psi[0, 0]
    renv = env_right[0, 0]
    pairs, width = x.shape[0], x.shape[2]
    count = float(nsec * pairs * width * width)

    env = env_build[0, 0]
    moved = from_behind(env)
    mpo = pair_mpo(site_left, site_right)
    x3 = front(x, renv, mpo)
    moved, x3 = lax.optimization_barrier((moved, x3))
    own = jnp.where(segment == 0, env, moved)

    core = sector % 2
    z = sector // 2
    chips = nsec // 2
    sign = 1 - 2 * core
    blocks = [own]
    holds = [sector]
    other = twin(own)
    blocks.append(other)
    holds.append(sector ^ 1)
    o, t = own, other
    for k in range(1, chips // 2 + 1):
        behind = (z - sign * k) % chips
        ahead = (z + sign * k) % chips
        o = hop(o)
        blocks += [o, twin(o)]
        holds += [2 * behind + core, 2 * ahead + 1 - core]
        if k < chips // 2:
            t = hop(t)
            blocks += [t, twin(t)]
            holds += [2 * behind + 1 - core, 2 * ahead + core]
    holds = jnp.stack(holds).astype(jnp.int32)
    left = (sector - charge) % nsec
    slot = jnp.sum(
        jnp.where(holds[None, :] == left[:, None], jnp.arange(nsec, dtype=jnp.int32)[None, :], 0), axis=1
    ).astype(jnp.int32)

    v, stat = back(slot, rank, x, renv, mpo, x3, blocks)

    mine = stat[1, 0]
    total = stat
    for bit in (1, 2, 4, 8):
        total = total + lax.ppermute(total, "sec", [(i, i ^ bit) for i in range(nsec)])
    scale_one = lax.rsqrt(total[0, 0] / count + 1e-06)
    energy = total[2, 0] / total[3, 0]
    second = (scale_one * scale_one) * total[1, 0]
    scale = scale_one * lax.rsqrt(second / count + 1e-06)
    state = (v * scale).astype(BF16)
    share = jnp.log(float(nsec) * mine / total[1, 0])
    upto = jnp.full((8, width), share, F32)
    whole = upto
    for bit in (1, 2, 4, 8):
        got = lax.ppermute(whole, "seg", [(i, i ^ bit) for i in range(nseg)])
        upto = jnp.where((segment & bit) != 0, upto + got, upto)
        whole = whole + got
    return state[None, None], energy.reshape(1), upto[0, 0].reshape(1, 1)


def solution(mesh):
    return jax.shard_map(
        shards,
        mesh=mesh,
        in_specs=(
            P("seg", "sec", None, None, None),
            P("seg", "sec", None, None, None),
            P("seg", "sec", None, None, None),
            P(),
            P(),
            P(),
            P("sec"),
        ),
        out_specs=(P("seg", "sec", None, None, None), P("seg"), P("seg", "sec")),
        check_vma=False,
    )
```

```python
import jax
import jax.numpy as jnp
import numpy as np
from jax import lax
from jax.experimental import pallas as pl
from jax.experimental.pallas import tpu as pltpu
from jax.sharding import PartitionSpec as P

F32 = jnp.float32
BF16 = jnp.bfloat16


LOCAL = 4
BLOCKS = 16
EARLY = 12
VMEM_LIMIT = 60 * 2**20


def iota(shape, dim):
    return lax.broadcasted_iota(jnp.int32, shape, dim)


def pair_mpo(left_ref, right_ref):
    rows, bonds = left_ref.shape
    pairs = LOCAL * LOCAL
    wide = 256
    over_w = (iota((bonds, wide), 0) == iota((bonds, wide), 1) // pairs).astype(BF16)
    big = jnp.dot(right_ref[...], over_w, preferred_element_type=F32)
    same = (iota((rows, wide), 0) % pairs) == (iota((rows, wide), 1) % pairs)
    big = jnp.where(same, big, 0.0).astype(BF16)
    by_m = (iota((16, rows), 0) == iota((16, rows), 1) // pairs).astype(BF16)
    right = jnp.dot(by_m, big, preferred_element_type=F32).astype(BF16)
    joined = jnp.dot(left_ref[...], right[:bonds], preferred_element_type=F32)
    gap = iota((rows, wide), 0) % LOCAL - (iota((rows, wide), 1) // LOCAL) % LOCAL
    out = jnp.zeros((rows, wide), F32)
    for d in range(1 - LOCAL, LOCAL):
        moved = pltpu.roll(pltpu.roll(joined, d % rows, 0), (-LOCAL * d) % wide, 1)
        out = jnp.where(gap == d, moved, out)
    return out[:, :rows].astype(BF16)


def turn(src_ref, xt_ref):
    for j in range(src_ref.shape[1] // 16):
        xt_ref[j * 16 : (j + 1) * 16] = jnp.swapaxes(src_ref[:, j * 16 : (j + 1) * 16, :], 0, 1)


def spread(xt_ref, renv_ref, mpo, x3_ref, done=None):
    states, pairs, width = xt_ref.shape
    bonds = renv_ref.shape[0]
    for at in range(0, states, 16):
        xa = xt_ref[at : at + 16].reshape(16 * pairs, width)
        first = []
        for k in range(bonds // 2):
            both = jnp.concatenate([renv_ref[2 * k], renv_ref[2 * k + 1]], axis=1)
            got = jnp.dot(xa, both, preferred_element_type=F32).astype(BF16)
            first += [got[:, :width], got[:, width:]]
        rows = []
        for i in range(8):
            sides = []
            for a in (2 * i, 2 * i + 1):
                sides.append(jnp.concatenate([f[a * pairs : (a + 1) * pairs] for f in first], axis=0))
            out = jnp.dot(mpo, jnp.concatenate(sides, axis=1), preferred_element_type=F32).astype(BF16)
            rows += [out[:, :width], out[:, width:]]
        for l in range(bonds):
            block = jnp.stack([row[l * pairs : (l + 1) * pairs] for row in rows], axis=0)
            x3_ref[:, l, at : at + 16, :] = jnp.swapaxes(block, 0, 1)
        if done is not None:
            done(at)


def front_kernel(psi_any, renv_any, left_ref, right_ref, x3_any, mpo_ref, psi_ref, renv_ref, xt_ref, x3_ref, sem_ref, out_sem):
    copies = [
        pltpu.make_async_copy(psi_any, psi_ref, sem_ref.at[0]),
        pltpu.make_async_copy(renv_any, renv_ref, sem_ref.at[1]),
    ]
    for copy in copies:
        copy.start()
    mpo = pair_mpo(left_ref, right_ref)
    mpo_ref[...] = mpo
    for copy in copies:
        copy.wait()
    turn(psi_ref, xt_ref)
    sent = []

    def done(at):
        rows = pl.ds(at, 16)
        sent.append(pltpu.make_async_copy(x3_ref.at[:, :, rows], x3_any.at[:, :, rows], out_sem.at[at // 16]))
        sent[-1].start()

    spread(xt_ref, renv_ref, mpo, x3_ref, done)
    for copy in sent:
        copy.wait()


def contract(lenv_ref, slot, x3_ref, q):
    bonds = lenv_ref.shape[1]
    total = None
    for k in range(bonds // 2):
        lhs = jnp.concatenate([lenv_ref[slot, 2 * k], lenv_ref[slot, 2 * k + 1]], axis=1)
        rhs = jnp.concatenate([x3_ref[q, 2 * k], x3_ref[q, 2 * k + 1]], axis=0)
        part = jnp.dot(lhs, rhs, preferred_element_type=F32)
        total = part if total is None else total + part
    return total


def masked_step(keep, psi_ref, u_ref, sq_ref, lenv_ref, slot, x3_ref, q):
    h = contract(lenv_ref, slot, x3_ref, q)
    u = jnp.where(keep, psi_ref[q].astype(F32) - 0.5 * h, 0.0)
    u_ref[q] = u.astype(BF16)
    sq_ref[...] += u * u


def mid_kernel(slot_ref, rank_ref, psi_any, x3_any, *rest):
    blocks = rest[:EARLY]
    u_ref, sq_ref, psi_ref, lenv_ref, x3_ref, sem_ref, x3_sem = rest[EARLY:]
    pairs, width = psi_ref.shape[0], psi_ref.shape[2]
    copies = [pltpu.make_async_copy(blocks[i], lenv_ref.at[i], sem_ref.at[i]) for i in range(EARLY)]
    copies.append(pltpu.make_async_copy(psi_any, psi_ref, sem_ref.at[EARLY]))
    for copy in copies:
        copy.start()
    loads = [pltpu.make_async_copy(x3_any.at[q], x3_ref.at[q], x3_sem.at[q]) for q in range(pairs)]
    for q in range(pairs):
        pl.when(slot_ref[q] < EARLY)(loads[q].start)
    keep = iota((width, width), 1) < rank_ref[0]
    sq_ref[...] = jnp.zeros_like(sq_ref)
    for copy in copies:
        copy.wait()
    for q in range(pairs):

        @pl.when(slot_ref[q] < EARLY)
        def _():
            loads[q].wait()
            masked_step(keep, psi_ref, u_ref, sq_ref, lenv_ref, slot_ref[q], x3_ref, q)

        @pl.when(slot_ref[q] >= EARLY)
        def _():
            u_ref[q] = jnp.zeros((width, width), BF16)


def back_kernel(slot_ref, rank_ref, psi_any, renv_any, mpo_ref, x3_any, early_u, early_sq, *rest):
    blocks = rest[:BLOCKS]
    v_any, stat_ref, lenv_ref, x3_ref, u_ref, xt_ref, psi_ref, renv_ref, v_ref, sq_ref = rest[BLOCKS:-3]
    sem_ref, x3_sem, v_sem = rest[-3:]
    pairs, width = psi_ref.shape[0], psi_ref.shape[2]
    copies = [pltpu.make_async_copy(blocks[i], lenv_ref.at[i], sem_ref.at[i]) for i in range(BLOCKS)]
    first = copies[EARLY:] + [
        pltpu.make_async_copy(psi_any, psi_ref, sem_ref.at[BLOCKS]),
        pltpu.make_async_copy(early_u, u_ref, sem_ref.at[BLOCKS + 1]),
    ]
    later = pltpu.make_async_copy(renv_any, renv_ref, sem_ref.at[BLOCKS + 2])
    loads = [pltpu.make_async_copy(x3_any.at[q], x3_ref.at[q], x3_sem.at[q]) for q in range(pairs)]
    for copy in first:
        copy.start()
    for q in range(pairs):
        pl.when(slot_ref[q] >= EARLY)(loads[q].start)
    later.start()
    for copy in copies[:EARLY]:
        copy.start()
    keep = iota((width, width), 1) < rank_ref[0]
    sq_ref[...] = early_sq[...]
    for copy in first:
        copy.wait()
    for q in range(pairs):

        @pl.when(slot_ref[q] >= EARLY)
        def _():
            loads[q].wait()
            masked_step(keep, psi_ref, u_ref, sq_ref, lenv_ref, slot_ref[q], x3_ref, q)

    turn(u_ref, xt_ref)
    later.wait()
    spread(xt_ref, renv_ref, mpo_ref[...], x3_ref)
    for copy in copies[:EARLY]:
        copy.wait()
    zero = jnp.zeros((width, width), F32)
    sq, inner, own = zero, zero, zero
    sent = []
    for q in range(pairs):
        h = contract(lenv_ref, slot_ref[q], x3_ref, q)
        x = u_ref[q].astype(F32)
        v = jnp.where(keep, x - 0.5 * h, 0.0)
        v_ref[q] = v
        sent.append(pltpu.make_async_copy(v_ref.at[q], v_any.at[q], v_sem.at[q]))
        sent[-1].start()
        sq, inner, own = sq + v * v, inner + x * h, own + x * x
    row = iota((8, width), 0)
    stat = jnp.zeros((8, width), F32)
    for i, part in enumerate((sq_ref[...], sq, inner, own)):
        stat = jnp.where(row == i, jnp.sum(part), stat)
    stat_ref[...] = stat
    for copy in sent:
        copy.wait()


VMEM_SPEC = pl.BlockSpec(memory_space=pltpu.VMEM)
SMEM_SPEC = pl.BlockSpec(memory_space=pltpu.SMEM)
ANY_SPEC = pl.BlockSpec(memory_space=pl.ANY)


def call(kernel, name, flops, out_shape, in_specs, out_specs, scratch):
    return pl.pallas_call(
        kernel,
        out_shape=out_shape,
        in_specs=in_specs,
        out_specs=out_specs,
        scratch_shapes=scratch,
        compiler_params=pltpu.CompilerParams(vmem_limit_bytes=VMEM_LIMIT),
        cost_estimate=pl.CostEstimate(flops=flops, bytes_accessed=8 * 10**6, transcendentals=0),
        name=name,
    )


def front(psi, renv, left, right):
    pairs, width = psi.shape[0], psi.shape[2]
    bonds = renv.shape[0]
    rows = bonds * pairs
    return call(
        front_kernel,
        "front",
        2 * 10**9,
        (jax.ShapeDtypeStruct((pairs, bonds, width, width), BF16), jax.ShapeDtypeStruct((rows, rows), BF16)),
        [ANY_SPEC, ANY_SPEC, VMEM_SPEC, VMEM_SPEC],
        (ANY_SPEC, VMEM_SPEC),
        [
            pltpu.VMEM((pairs, width, width), BF16),
            pltpu.VMEM((bonds, width, width), BF16),
            pltpu.VMEM((width, pairs, width), BF16),
            pltpu.VMEM((pairs, bonds, width, width), BF16),
            pltpu.SemaphoreType.DMA((2,)),
            pltpu.SemaphoreType.DMA((width // 16,)),
        ],
    )(psi, renv, left, right)


def mid(slot, rank, psi, x3, blocks):
    pairs, width = psi.shape[0], psi.shape[2]
    bonds = x3.shape[1]
    return call(
        mid_kernel,
        "mid",
        10**9,
        (jax.ShapeDtypeStruct((pairs, width, width), BF16), jax.ShapeDtypeStruct((width, width), F32)),
        [SMEM_SPEC, SMEM_SPEC, ANY_SPEC, ANY_SPEC] + [ANY_SPEC] * EARLY,
        (VMEM_SPEC, VMEM_SPEC),
        [
            pltpu.VMEM((pairs, width, width), BF16),
            pltpu.VMEM((EARLY, bonds, width, width), BF16),
            pltpu.VMEM((pairs, bonds, width, width), BF16),
            pltpu.SemaphoreType.DMA((EARLY + 1,)),
            pltpu.SemaphoreType.DMA((pairs,)),
        ],
    )(slot, rank, psi, x3, *blocks)


def back(slot, rank, psi, renv, mpo, x3, early_u, early_sq, blocks):
    pairs, width = psi.shape[0], psi.shape[2]
    bonds = renv.shape[0]
    return call(
        back_kernel,
        "back",
        3 * 10**9,
        (jax.ShapeDtypeStruct((pairs, width, width), F32), jax.ShapeDtypeStruct((8, width), F32)),
        [SMEM_SPEC, SMEM_SPEC, ANY_SPEC, ANY_SPEC, VMEM_SPEC, ANY_SPEC, ANY_SPEC, VMEM_SPEC] + [ANY_SPEC] * BLOCKS,
        (ANY_SPEC, VMEM_SPEC),
        [
            pltpu.VMEM((BLOCKS, bonds, width, width), BF16),
            pltpu.VMEM((pairs, bonds, width, width), BF16),
            pltpu.VMEM((pairs, width, width), BF16),
            pltpu.VMEM((width, pairs, width), BF16),
            pltpu.VMEM((pairs, width, width), BF16),
            pltpu.VMEM((bonds, width, width), BF16),
            pltpu.VMEM((pairs, width, width), F32),
            pltpu.VMEM((width, width), F32),
            pltpu.SemaphoreType.DMA((BLOCKS + 3,)),
            pltpu.SemaphoreType.DMA((pairs,)),
            pltpu.SemaphoreType.DMA((pairs,)),
        ],
    )(slot, rank, psi, renv, mpo, x3, early_u, early_sq, *blocks)


def hop(value):
    n = lax.axis_size("sec")
    return lax.ppermute(value, "sec", [(i, (i + (2 if i % 2 == 0 else -2)) % n) for i in range(n)])


def cross_hop(value):
    n = lax.axis_size("sec")
    return lax.ppermute(value, "sec", [(i, (i + (-2 if i % 2 == 0 else 2)) % n ^ 1) for i in range(n)])


def twin(value):
    n = lax.axis_size("sec")
    return lax.ppermute(value, "sec", [(i, i ^ 1) for i in range(n)])


def from_behind(value):
    n = lax.axis_size("seg")
    return lax.ppermute(value, "seg", [(i, i + 1) for i in range(n - 1)])


def shards(psi, env_build, env_right, site_left, site_right, charge, rank):
    nsec = lax.axis_size("sec")
    nseg = lax.axis_size("seg")
    sector = lax.axis_index("sec")
    segment = lax.axis_index("seg")
    x = psi[0, 0]
    renv = env_right[0, 0]
    pairs, width = x.shape[0], x.shape[2]
    count = float(nsec * pairs * width * width)

    env = env_build[0, 0]
    moved = from_behind(env)
    tall = (site_left.shape[0] * pairs, site_left.shape[1])
    x3, mpo = front(
        x, renv, site_left.transpose(0, 2, 3, 1).reshape(tall), site_right.transpose(0, 2, 3, 1).reshape(tall)
    )
    moved, x3 = lax.optimization_barrier((moved, x3))
    own = jnp.where(segment == 0, env, moved)

    chips = nsec // 2
    held = np.zeros((nsec, nsec), np.int32)
    for s in range(nsec):
        z, c = s // 2, s % 2
        sign = 1 - 2 * c
        order = [s, s ^ 1]
        for k in range(1, chips // 2 + 1):
            behind, ahead = (z - sign * k) % chips, (z + sign * k) % chips
            t_pair = [2 * behind + 1 - c, 2 * ahead + c] if k < chips // 2 else []
            o_pair = [2 * behind + c, 2 * ahead + 1 - c]
            order += o_pair + t_pair
        for i, left in enumerate(order):
            held[s, left] = i
    row = lax.dynamic_index_in_dim(jnp.asarray(held), sector, 0, keepdims=False)
    left = (sector - charge) % nsec
    hits = left[:, None] == jnp.arange(nsec, dtype=jnp.int32)[None, :]
    slot = jnp.sum(jnp.where(hits, row[None, :], 0), axis=1).astype(jnp.int32)

    o1, t1 = hop(own), cross_hop(own)
    o2, t2 = hop(o1), hop(t1)
    o3, t3 = hop(o2), hop(t2)
    o4 = hop(o3)
    blocks = [own, twin(own), o1, twin(o1), t1, twin(t1), o2, twin(o2), t2, twin(t2), o3, twin(o3)]
    early_u, early_sq = mid(slot, rank, x, x3, blocks)
    t3, early_u = lax.optimization_barrier((t3, early_u))
    blocks += [t3, twin(t3), o4, twin(o4)]

    v, stat = back(slot, rank, x, renv, mpo, x3, early_u, early_sq, blocks)

    mine = stat[1, 0]
    total = stat
    for bit in (1, 2, 4, 8):
        total = total + lax.ppermute(total, "sec", [(i, i ^ bit) for i in range(nsec)])
    scale_one = lax.rsqrt(total[0, 0] / count + 1e-06)
    energy = total[2, 0] / total[3, 0]
    second = (scale_one * scale_one) * total[1, 0]
    scale = scale_one * lax.rsqrt(second / count + 1e-06)
    state = (v * scale).astype(BF16)
    share = jnp.log(float(nsec) * mine / total[1, 0])
    upto = jnp.full((8, width), share, F32)
    whole = upto
    for bit in (1, 2, 4, 8):
        got = lax.ppermute(whole, "seg", [(i, i ^ bit) for i in range(nseg)])
        upto = jnp.where((segment & bit) != 0, upto + got, upto)
        whole = whole + got
    return state[None, None], energy.reshape(1), upto[0, 0].reshape(1, 1)


def solution(mesh):
    return jax.shard_map(
        shards,
        mesh=mesh,
        in_specs=(
            P("seg", "sec", None, None, None),
            P("seg", "sec", None, None, None),
            P("seg", "sec", None, None, None),
            P(),
            P(),
            P(),
            P("sec"),
        ),
        out_specs=(P("seg", "sec", None, None, None), P("seg"), P("seg", "sec")),
        check_vma=False,
    )
```

```python
import functools

import jax
import jax.numpy as jnp
from jax import lax
from jax.experimental import pallas as pl
from jax.experimental.pallas import tpu as pltpu
from jax.sharding import PartitionSpec as P

F32 = jnp.float32
BF16 = jnp.bfloat16


LOCAL = 4
BLOCKS = 16
LATE = range(8, 12)
VMEM_LIMIT = 60 * 2**20


def iota(shape, dim):
    return lax.broadcasted_iota(jnp.int32, shape, dim)


def pair_mpo(left_ref, right_ref):
    rows, bonds = left_ref.shape
    pairs = LOCAL * LOCAL
    wide = 256
    over_w = (iota((bonds, wide), 0) == iota((bonds, wide), 1) // pairs).astype(BF16)
    big = jnp.dot(right_ref[...], over_w, preferred_element_type=F32)
    same = (iota((rows, wide), 0) % pairs) == (iota((rows, wide), 1) % pairs)
    big = jnp.where(same, big, 0.0).astype(BF16)
    by_m = (iota((16, rows), 0) == iota((16, rows), 1) // pairs).astype(BF16)
    right = jnp.dot(by_m, big, preferred_element_type=F32).astype(BF16)
    joined = jnp.dot(left_ref[...], right[:bonds], preferred_element_type=F32)
    gap = iota((rows, wide), 0) % LOCAL - (iota((rows, wide), 1) // LOCAL) % LOCAL
    out = jnp.zeros((rows, wide), F32)
    for d in range(1 - LOCAL, LOCAL):
        moved = pltpu.roll(pltpu.roll(joined, d % rows, 0), (-LOCAL * d) % wide, 1)
        out = jnp.where(gap == d, moved, out)
    return out[:, :rows].astype(BF16)


def turn(src_ref, xt_ref):
    for j in range(src_ref.shape[1] // 16):
        xt_ref[j * 16 : (j + 1) * 16] = jnp.swapaxes(src_ref[:, j * 16 : (j + 1) * 16, :], 0, 1)


def spread(xt_ref, renv_ref, mpo, x3_ref, done=None):
    states, pairs, width = xt_ref.shape
    bonds = renv_ref.shape[0]
    for at in range(0, states, 16):
        xa = xt_ref[at : at + 16].reshape(16 * pairs, width)
        first = []
        for k in range(bonds // 2):
            both = jnp.concatenate([renv_ref[2 * k], renv_ref[2 * k + 1]], axis=1)
            got = jnp.dot(xa, both, preferred_element_type=F32).astype(BF16)
            first += [got[:, :width], got[:, width:]]
        rows = []
        for i in range(8):
            sides = []
            for a in (2 * i, 2 * i + 1):
                sides.append(jnp.concatenate([f[a * pairs : (a + 1) * pairs] for f in first], axis=0))
            out = jnp.dot(mpo, jnp.concatenate(sides, axis=1), preferred_element_type=F32).astype(BF16)
            rows += [out[:, :width], out[:, width:]]
        for l in range(bonds):
            block = jnp.stack([row[l * pairs : (l + 1) * pairs] for row in rows], axis=0)
            x3_ref[:, l, at : at + 16, :] = jnp.swapaxes(block, 0, 1)
        if done is not None:
            done(at)


def front_kernel(psi_any, renv_any, left_ref, right_ref, x3_any, mpo_ref, psi_ref, renv_ref, xt_ref, x3_ref, sem_ref, out_sem):
    copies = [
        pltpu.make_async_copy(psi_any, psi_ref, sem_ref.at[0]),
        pltpu.make_async_copy(renv_any, renv_ref, sem_ref.at[1]),
    ]
    for copy in copies:
        copy.start()
    mpo = pair_mpo(left_ref, right_ref)
    mpo_ref[...] = mpo
    for copy in copies:
        copy.wait()
    turn(psi_ref, xt_ref)
    sent = []

    def done(at):
        rows = pl.ds(at, 16)
        sent.append(pltpu.make_async_copy(x3_ref.at[:, :, rows], x3_any.at[:, :, rows], out_sem.at[at // 16]))
        sent[-1].start()

    spread(xt_ref, renv_ref, mpo, x3_ref, done)
    for copy in sent:
        copy.wait()


def contract(lenv_ref, slot, x3_ref, q):
    bonds = lenv_ref.shape[1]
    total = None
    for k in range(bonds // 2):
        lhs = jnp.concatenate([lenv_ref[slot, 2 * k], lenv_ref[slot, 2 * k + 1]], axis=1)
        rhs = jnp.concatenate([x3_ref[q, 2 * k], x3_ref[q, 2 * k + 1]], axis=0)
        part = jnp.dot(lhs, rhs, preferred_element_type=F32)
        total = part if total is None else total + part
    return total


def slot_of(charge_ref, q):
    sector = lax.axis_index("sec")
    left = (sector - charge_ref[q]) & 15
    core = sector & 1
    ahead = (sector >> 1) - (left >> 1)
    hops = jnp.where(core == 0, ahead, -ahead) & 7
    return 2 * hops + ((left ^ sector) & 1)


def is_late(slot):
    return jnp.logical_and(slot >= LATE.start, slot < LATE.stop)


def masked_step(keep, psi_ref, u_ref, sq_ref, lenv_ref, slot, x3_ref, q):
    h = contract(lenv_ref, slot, x3_ref, q)
    u = jnp.where(keep, psi_ref[q].astype(F32) - 0.5 * h, 0.0)
    u_ref[q] = u.astype(BF16)
    sq_ref[...] += u * u


def mid_kernel(charge_ref, rank_ref, psi_any, x3_any, *rest):
    early = [i for i in range(BLOCKS) if i not in LATE]
    blocks = rest[: len(early)]
    u_ref, sq_ref, psi_ref, lenv_ref, x3_ref, sem_ref, x3_sem = rest[len(early) :]
    pairs, width = psi_ref.shape[0], psi_ref.shape[2]
    copies = [pltpu.make_async_copy(b, lenv_ref.at[i], sem_ref.at[i]) for i, b in zip(early, blocks)]
    copies.append(pltpu.make_async_copy(psi_any, psi_ref, sem_ref.at[BLOCKS]))
    for copy in copies:
        copy.start()
    slots = [slot_of(charge_ref, q) for q in range(pairs)]
    loads = [pltpu.make_async_copy(x3_any.at[q], x3_ref.at[q], x3_sem.at[q]) for q in range(pairs)]
    for q in range(pairs):
        pl.when(jnp.logical_not(is_late(slots[q])))(loads[q].start)
    keep = iota((width, width), 1) < rank_ref[0]
    sq_ref[...] = jnp.zeros_like(sq_ref)
    for copy in copies:
        copy.wait()
    for q in range(pairs):

        @pl.when(jnp.logical_not(is_late(slots[q])))
        def _():
            loads[q].wait()
            masked_step(keep, psi_ref, u_ref, sq_ref, lenv_ref, slots[q], x3_ref, q)

        @pl.when(is_late(slots[q]))
        def _():
            u_ref[q] = jnp.zeros((width, width), BF16)


def back_kernel(charge_ref, rank_ref, psi_any, renv_any, mpo_ref, x3_any, early_u, early_sq, *rest):
    blocks = rest[:BLOCKS]
    v_any, stat_ref, lenv_ref, x3_ref, u_ref, xt_ref, psi_ref, renv_ref, v_ref, sq_ref = rest[BLOCKS:-3]
    sem_ref, x3_sem, v_sem = rest[-3:]
    pairs, width = psi_ref.shape[0], psi_ref.shape[2]
    copies = [pltpu.make_async_copy(blocks[i], lenv_ref.at[i], sem_ref.at[i]) for i in range(BLOCKS)]
    first = [copies[i] for i in LATE] + [
        pltpu.make_async_copy(psi_any, psi_ref, sem_ref.at[BLOCKS]),
        pltpu.make_async_copy(early_u, u_ref, sem_ref.at[BLOCKS + 1]),
    ]
    later = pltpu.make_async_copy(renv_any, renv_ref, sem_ref.at[BLOCKS + 2])
    last = [copies[i] for i in range(BLOCKS) if i not in LATE]
    slots = [slot_of(charge_ref, q) for q in range(pairs)]
    loads = [pltpu.make_async_copy(x3_any.at[q], x3_ref.at[q], x3_sem.at[q]) for q in range(pairs)]
    for copy in first:
        copy.start()
    for q in range(pairs):
        pl.when(is_late(slots[q]))(loads[q].start)
    later.start()
    keep = iota((width, width), 1) < rank_ref[0]
    sq_ref[...] = early_sq[...]
    for copy in first:
        copy.wait()
    for copy in last:
        copy.start()
    for q in range(pairs):

        @pl.when(is_late(slots[q]))
        def _():
            loads[q].wait()
            masked_step(keep, psi_ref, u_ref, sq_ref, lenv_ref, slots[q], x3_ref, q)

    turn(u_ref, xt_ref)
    later.wait()
    spread(xt_ref, renv_ref, mpo_ref[...], x3_ref)
    for copy in last:
        copy.wait()
    zero = jnp.zeros((width, width), F32)
    sq, inner, own = zero, zero, zero
    sent = []
    for q in range(pairs):
        h = contract(lenv_ref, slots[q], x3_ref, q)
        x = u_ref[q].astype(F32)
        v = jnp.where(keep, x - 0.5 * h, 0.0)
        v_ref[q] = v
        sent.append(pltpu.make_async_copy(v_ref.at[q], v_any.at[q], v_sem.at[q]))
        sent[-1].start()
        sq, inner, own = sq + v * v, inner + x * h, own + x * x
    for i, part in enumerate((sq_ref[...], sq, inner, own)):
        stat_ref[i : i + 1] = jnp.sum(part, axis=0, keepdims=True)
    for copy in sent:
        copy.wait()


def settle_kernel(count, total_ref, mine_ref, twin_ref, share_ref, out_ref):
    width = total_ref.shape[1]
    first_sq, sq, inner, own = [jnp.sum(total_ref[i : i + 1], axis=1, keepdims=True) for i in range(4)]
    one = lax.rsqrt(first_sq / count + 1e-06)
    scale = one * lax.rsqrt(one * one * sq / count + 1e-06)
    row = iota((8, width), 0)
    out_ref[...] = jnp.where(row == 0, scale, inner / own)
    mine = jnp.sum(mine_ref[1:2], axis=1, keepdims=True)
    twin = jnp.sum(twin_ref[1:2], axis=1, keepdims=True)
    row = iota((2, width), 0)
    here = jnp.where(row == (lax.axis_index("sec") & 1), mine, twin)
    share = jnp.log(float(lax.axis_size("sec")) * here / sq)
    share_ref[...] = jnp.where(iota((2, width), 1) == lax.axis_index("seg"), share, 0.0)


VMEM_SPEC = pl.BlockSpec(memory_space=pltpu.VMEM)
SMEM_SPEC = pl.BlockSpec(memory_space=pltpu.SMEM)
ANY_SPEC = pl.BlockSpec(memory_space=pl.ANY)


def call(kernel, name, flops, out_shape, in_specs, out_specs, scratch):
    return pl.pallas_call(
        kernel,
        out_shape=out_shape,
        in_specs=in_specs,
        out_specs=out_specs,
        scratch_shapes=scratch,
        compiler_params=pltpu.CompilerParams(vmem_limit_bytes=VMEM_LIMIT),
        cost_estimate=pl.CostEstimate(flops=flops, bytes_accessed=8 * 10**6, transcendentals=0),
        name=name,
    )


def front(psi, renv, left, right):
    pairs, width = psi.shape[0], psi.shape[2]
    bonds = renv.shape[0]
    rows = bonds * pairs
    return call(
        front_kernel,
        "front",
        2 * 10**9,
        (jax.ShapeDtypeStruct((pairs, bonds, width, width), BF16), jax.ShapeDtypeStruct((rows, rows), BF16)),
        [ANY_SPEC, ANY_SPEC, VMEM_SPEC, VMEM_SPEC],
        (ANY_SPEC, VMEM_SPEC),
        [
            pltpu.VMEM((pairs, width, width), BF16),
            pltpu.VMEM((bonds, width, width), BF16),
            pltpu.VMEM((width, pairs, width), BF16),
            pltpu.VMEM((pairs, bonds, width, width), BF16),
            pltpu.SemaphoreType.DMA((2,)),
            pltpu.SemaphoreType.DMA((width // 16,)),
        ],
    )(psi, renv, left, right)


def mid(charge, rank, psi, x3, blocks):
    pairs, width = psi.shape[0], psi.shape[2]
    bonds = x3.shape[1]
    return call(
        mid_kernel,
        "mid",
        10**9,
        (jax.ShapeDtypeStruct((pairs, width, width), BF16), jax.ShapeDtypeStruct((width, width), F32)),
        [SMEM_SPEC, SMEM_SPEC, ANY_SPEC, ANY_SPEC] + [ANY_SPEC] * len(blocks),
        (VMEM_SPEC, VMEM_SPEC),
        [
            pltpu.VMEM((pairs, width, width), BF16),
            pltpu.VMEM((BLOCKS, bonds, width, width), BF16),
            pltpu.VMEM((pairs, bonds, width, width), BF16),
            pltpu.SemaphoreType.DMA((BLOCKS + 1,)),
            pltpu.SemaphoreType.DMA((pairs,)),
        ],
    )(charge, rank, psi, x3, *blocks)


def back(charge, rank, psi, renv, mpo, x3, early_u, early_sq, blocks):
    pairs, width = psi.shape[0], psi.shape[2]
    bonds = renv.shape[0]
    return call(
        back_kernel,
        "back",
        3 * 10**9,
        (jax.ShapeDtypeStruct((pairs, width, width), F32), jax.ShapeDtypeStruct((4, width), F32)),
        [SMEM_SPEC, SMEM_SPEC, ANY_SPEC, ANY_SPEC, VMEM_SPEC, ANY_SPEC, ANY_SPEC, VMEM_SPEC] + [ANY_SPEC] * BLOCKS,
        (ANY_SPEC, VMEM_SPEC),
        [
            pltpu.VMEM((BLOCKS, bonds, width, width), BF16),
            pltpu.VMEM((pairs, bonds, width, width), BF16),
            pltpu.VMEM((pairs, width, width), BF16),
            pltpu.VMEM((width, pairs, width), BF16),
            pltpu.VMEM((pairs, width, width), BF16),
            pltpu.VMEM((bonds, width, width), BF16),
            pltpu.VMEM((pairs, width, width), F32),
            pltpu.VMEM((width, width), F32),
            pltpu.SemaphoreType.DMA((BLOCKS + 3,)),
            pltpu.SemaphoreType.DMA((pairs,)),
            pltpu.SemaphoreType.DMA((pairs,)),
        ],
    )(charge, rank, psi, renv, mpo, x3, early_u, early_sq, *blocks)


def settle(total, mine, twin_stat, count):
    width = total.shape[1]
    return call(
        functools.partial(settle_kernel, count),
        "settle",
        10**4,
        (jax.ShapeDtypeStruct((2, width), F32), jax.ShapeDtypeStruct((8, width), F32)),
        [VMEM_SPEC] * 3,
        (VMEM_SPEC, VMEM_SPEC),
        [],
    )(total, mine, twin_stat)


def partner(value, bits):
    axes = ("seg", "sec")
    n = lax.axis_size(axes)
    return lax.ppermute(value, axes, [(i, i ^ bits) for i in range(n)])


def hop(value):
    n = lax.axis_size("sec")
    return lax.ppermute(value, "sec", [(i, (i + (2 if i % 2 == 0 else -2)) % n) for i in range(n)])


def cross_hop(value):
    n = lax.axis_size("sec")
    return lax.ppermute(value, "sec", [(i, (i + (-2 if i % 2 == 0 else 2)) % n ^ 1) for i in range(n)])


def twin(value):
    n = lax.axis_size("sec")
    return lax.ppermute(value, "sec", [(i, i ^ 1) for i in range(n)])


def from_behind(value):
    n = lax.axis_size("seg")
    return lax.ppermute(value, "seg", [(i, i + 1) for i in range(n - 1)])


def shards(psi, env_build, env_right, site_left, site_right, charge, rank):
    nsec = lax.axis_size("sec")
    sector = lax.axis_index("sec")
    segment = lax.axis_index("seg")
    x = psi[0, 0]
    renv = env_right[0, 0]
    pairs, width = x.shape[0], x.shape[2]
    count = float(nsec * pairs * width * width)

    env = env_build[0, 0]
    moved = from_behind(env)
    tall = (site_left.shape[0] * pairs, site_left.shape[1])
    x3, mpo = front(
        x, renv, site_left.transpose(0, 2, 3, 1).reshape(tall), site_right.transpose(0, 2, 3, 1).reshape(tall)
    )
    moved, x3 = lax.optimization_barrier((moved, x3))
    own = jnp.where(segment == 0, env, moved)

    o1, t1 = lax.optimization_barrier((hop(own), cross_hop(own)))
    o2, t2 = lax.optimization_barrier((hop(o1), hop(t1)))
    o3, t3 = lax.optimization_barrier((hop(o2), hop(t2)))
    o4 = hop(o3)
    near = [own, twin(own), o1, t1, o2, t2, o3, t3]
    far = [twin(t2), twin(o2), twin(t1), twin(o1)]
    early_u, early_sq = mid(charge, rank, x, x3, near + far)
    o4, early_u = lax.optimization_barrier((o4, early_u))
    blocks = near + [o4, twin(o4), twin(t3), twin(o3)] + far
    v, stat = back(charge, rank, x, renv, mpo, x3, early_u, early_sq, blocks)

    twin_stat = partner(stat, 1)
    total = stat + twin_stat
    for bits in (3, 5, 13):
        total = total + partner(total, bits)
    share, out = settle(total, stat, twin_stat, count)
    state = (v * out[0, 0]).astype(BF16)
    for bits in (1, 3, 4, 12):
        share = share + partner(share, nsec * bits + 1)
    wanted = (iota(share.shape, 0) == sector % 2) & (iota(share.shape, 1) <= segment)
    weight = jnp.sum(jnp.where(wanted, share, 0.0))
    return state[None, None], out[1:2, 0], weight.reshape(1, 1)


def solution(mesh):
    return jax.shard_map(
        shards,
        mesh=mesh,
        in_specs=(
            P("seg", "sec", None, None, None),
            P("seg", "sec", None, None, None),
            P("seg", "sec", None, None, None),
            P(),
            P(),
            P(),
            P("sec"),
        ),
        out_specs=(P("seg", "sec", None, None, None), P("seg"), P("seg", "sec")),
        check_vma=False,
    )
```

```python
import functools

import jax
import jax.numpy as jnp
from jax import lax
from jax.experimental import pallas as pl
from jax.experimental.pallas import tpu as pltpu
from jax.sharding import PartitionSpec as P

F32 = jnp.float32
BF16 = jnp.bfloat16


LOCAL = 4
BLOCKS = 16
VMEM_LIMIT = 60 * 2**20


def iota(shape, dim):
    return lax.broadcasted_iota(jnp.int32, shape, dim)


def pair_mpo(left_ref, right_ref):
    rows, bonds = left_ref.shape
    pairs = LOCAL * LOCAL
    wide = 256
    over_w = (iota((bonds, wide), 0) == iota((bonds, wide), 1) // pairs).astype(BF16)
    big = jnp.dot(right_ref[...], over_w, preferred_element_type=F32)
    same = (iota((rows, wide), 0) % pairs) == (iota((rows, wide), 1) % pairs)
    big = jnp.where(same, big, 0.0).astype(BF16)
    by_m = (iota((16, rows), 0) == iota((16, rows), 1) // pairs).astype(BF16)
    right = jnp.dot(by_m, big, preferred_element_type=F32).astype(BF16)
    joined = jnp.dot(left_ref[...], right[:bonds], preferred_element_type=F32)
    gap = iota((rows, wide), 0) % LOCAL - (iota((rows, wide), 1) // LOCAL) % LOCAL
    out = jnp.zeros((rows, wide), F32)
    for d in range(1 - LOCAL, LOCAL):
        moved = pltpu.roll(pltpu.roll(joined, d % rows, 0), (-LOCAL * d) % wide, 1)
        out = jnp.where(gap == d, moved, out)
    return out[:, :rows].astype(BF16)


def turn(src_ref, xt_ref):
    for j in range(src_ref.shape[1] // 16):
        xt_ref[j * 16 : (j + 1) * 16] = jnp.swapaxes(src_ref[:, j * 16 : (j + 1) * 16, :], 0, 1)


def spread(xt_ref, renv_ref, mpo, x3_ref, done=None):
    states, pairs, width = xt_ref.shape
    bonds = renv_ref.shape[0]
    for at in range(0, states, 16):
        xa = xt_ref[at : at + 16].reshape(16 * pairs, width)
        first = []
        for k in range(bonds // 2):
            both = jnp.concatenate([renv_ref[2 * k], renv_ref[2 * k + 1]], axis=1)
            got = jnp.dot(xa, both, preferred_element_type=F32).astype(BF16)
            first += [got[:, :width], got[:, width:]]
        rows = []
        for i in range(8):
            sides = []
            for a in (2 * i, 2 * i + 1):
                sides.append(jnp.concatenate([f[a * pairs : (a + 1) * pairs] for f in first], axis=0))
            out = jnp.dot(mpo, jnp.concatenate(sides, axis=1), preferred_element_type=F32).astype(BF16)
            rows += [out[:, :width], out[:, width:]]
        for l in range(bonds):
            block = jnp.stack([row[l * pairs : (l + 1) * pairs] for row in rows], axis=0)
            x3_ref[:, l, at : at + 16, :] = jnp.swapaxes(block, 0, 1)
        if done is not None:
            done(at)


def front_kernel(start, psi_any, renv_any, left_ref, right_ref, x3_any, mpo_ref, psi_ref, renv_ref, xt_ref, x3_ref, sem_ref, out_sem):
    copies = [
        pltpu.make_async_copy(psi_any.at[:, pl.ds(start, psi_ref.shape[1])], psi_ref, sem_ref.at[0]),
        pltpu.make_async_copy(renv_any, renv_ref, sem_ref.at[1]),
    ]
    for copy in copies:
        copy.start()
    mpo = pair_mpo(left_ref, right_ref)
    mpo_ref[...] = mpo
    for copy in copies:
        copy.wait()
    turn(psi_ref, xt_ref)
    sent = []

    def done(at):
        rows = pl.ds(at, 16)
        sent.append(pltpu.make_async_copy(x3_ref.at[:, :, rows], x3_any.at[:, :, rows], out_sem.at[at // 16]))
        sent[-1].start()

    spread(xt_ref, renv_ref, mpo, x3_ref, done)
    for copy in sent:
        copy.wait()


def contract(lenv_ref, slot, x3_ref, q):
    bonds = lenv_ref.shape[1]
    total = None
    for k in range(bonds // 2):
        lhs = jnp.concatenate([lenv_ref[slot, 2 * k], lenv_ref[slot, 2 * k + 1]], axis=1)
        rhs = jnp.concatenate([x3_ref[q, 2 * k], x3_ref[q, 2 * k + 1]], axis=0)
        part = jnp.dot(lhs, rhs, preferred_element_type=F32)
        total = part if total is None else total + part
    return total


def slot_of(charge_ref, q):
    sector = lax.axis_index("sec")
    left = (sector - charge_ref[q]) & 15
    core = sector & 1
    ahead = (sector >> 1) - (left >> 1)
    hops = jnp.where(core == 0, ahead, -ahead) & 7
    return 2 * hops + ((left ^ sector) & 1)


def back_kernel(charge_ref, rank_ref, psi_any, renv_any, mpo_ref, x3_low, x3_high, *rest):
    blocks = rest[:BLOCKS]
    v_any, stat_ref, lenv_ref, x3_ref, u_ref, xt_ref, psi_ref, renv_ref, v_ref = rest[BLOCKS:-3]
    sem_ref, x3_sem, v_sem = rest[-3:]
    pairs, width = psi_ref.shape[0], psi_ref.shape[2]
    half = x3_low.shape[2]
    first = [pltpu.make_async_copy(blocks[i], lenv_ref.at[i], sem_ref.at[i]) for i in range(BLOCKS)]
    first.append(pltpu.make_async_copy(psi_any, psi_ref, sem_ref.at[BLOCKS]))
    later = pltpu.make_async_copy(renv_any, renv_ref, sem_ref.at[BLOCKS + 1])
    loads = []
    for q in range(pairs):
        loads.append(
            (
                pltpu.make_async_copy(x3_low.at[q], x3_ref.at[q, :, pl.ds(0, half)], x3_sem.at[0, q]),
                pltpu.make_async_copy(x3_high.at[q], x3_ref.at[q, :, pl.ds(half, half)], x3_sem.at[1, q]),
            )
        )
    for copy in first:
        copy.start()
    for low, high in loads:
        low.start()
        high.start()
    later.start()
    slots = [slot_of(charge_ref, q) for q in range(pairs)]
    keep = iota((width, width), 1) < rank_ref[0]
    zero = jnp.zeros((width, width), F32)
    for copy in first:
        copy.wait()
    first_sq = zero
    for q in range(pairs):
        loads[q][0].wait()
        loads[q][1].wait()
        h = contract(lenv_ref, slots[q], x3_ref, q)
        u = jnp.where(keep, psi_ref[q].astype(F32) - 0.5 * h, 0.0)
        u_ref[q] = u.astype(BF16)
        first_sq = first_sq + u * u
    later.wait()
    turn(u_ref, xt_ref)
    spread(xt_ref, renv_ref, mpo_ref[...], x3_ref)
    sq, inner, own = zero, zero, zero
    sent = []
    for q in range(pairs):
        h = contract(lenv_ref, slots[q], x3_ref, q)
        x = u_ref[q].astype(F32)
        v = jnp.where(keep, x - 0.5 * h, 0.0)
        v_ref[q] = v
        sent.append(pltpu.make_async_copy(v_ref.at[q], v_any.at[q], v_sem.at[q]))
        sent[-1].start()
        sq, inner, own = sq + v * v, inner + x * h, own + x * x
    for i, part in enumerate((first_sq, sq, inner, own)):
        stat_ref[i : i + 1] = jnp.sum(part, axis=0, keepdims=True)
    for copy in sent:
        copy.wait()


def settle_kernel(count, total_ref, mine_ref, twin_ref, share_ref, out_ref):
    width = total_ref.shape[1]
    first_sq, sq, inner, own = [jnp.sum(total_ref[i : i + 1], axis=1, keepdims=True) for i in range(4)]
    one = lax.rsqrt(first_sq / count + 1e-06)
    scale = one * lax.rsqrt(one * one * sq / count + 1e-06)
    row = iota((8, width), 0)
    out_ref[...] = jnp.where(row == 0, scale, inner / own)
    mine = jnp.sum(mine_ref[1:2], axis=1, keepdims=True)
    twin = jnp.sum(twin_ref[1:2], axis=1, keepdims=True)
    row = iota((2, width), 0)
    here = jnp.where(row == (lax.axis_index("sec") & 1), mine, twin)
    share = jnp.log(float(lax.axis_size("sec")) * here / sq)
    share_ref[...] = jnp.where(iota((2, width), 1) == lax.axis_index("seg"), share, 0.0)


VMEM_SPEC = pl.BlockSpec(memory_space=pltpu.VMEM)
SMEM_SPEC = pl.BlockSpec(memory_space=pltpu.SMEM)
ANY_SPEC = pl.BlockSpec(memory_space=pl.ANY)


def call(kernel, name, flops, out_shape, in_specs, out_specs, scratch):
    return pl.pallas_call(
        kernel,
        out_shape=out_shape,
        in_specs=in_specs,
        out_specs=out_specs,
        scratch_shapes=scratch,
        compiler_params=pltpu.CompilerParams(vmem_limit_bytes=VMEM_LIMIT),
        cost_estimate=pl.CostEstimate(flops=flops, bytes_accessed=8 * 10**6, transcendentals=0),
        name=name,
    )


def front(psi, renv, left, right, part, parts):
    pairs, width = psi.shape[0], psi.shape[2]
    states = width // parts
    bonds = renv.shape[0]
    rows = bonds * pairs
    return call(
        functools.partial(front_kernel, part * states),
        "front",
        2 * 10**9 // parts,
        (jax.ShapeDtypeStruct((pairs, bonds, states, width), BF16), jax.ShapeDtypeStruct((rows, rows), BF16)),
        [ANY_SPEC, ANY_SPEC, VMEM_SPEC, VMEM_SPEC],
        (ANY_SPEC, VMEM_SPEC),
        [
            pltpu.VMEM((pairs, states, width), BF16),
            pltpu.VMEM((bonds, width, width), BF16),
            pltpu.VMEM((states, pairs, width), BF16),
            pltpu.VMEM((pairs, bonds, states, width), BF16),
            pltpu.SemaphoreType.DMA((2,)),
            pltpu.SemaphoreType.DMA((states // 16,)),
        ],
    )(psi, renv, left, right)


def back(charge, rank, psi, renv, mpo, x3_low, x3_high, blocks):
    pairs, width = psi.shape[0], psi.shape[2]
    bonds = renv.shape[0]
    return call(
        back_kernel,
        "back",
        4 * 10**9,
        (jax.ShapeDtypeStruct((pairs, width, width), F32), jax.ShapeDtypeStruct((4, width), F32)),
        [SMEM_SPEC, SMEM_SPEC, ANY_SPEC, ANY_SPEC, VMEM_SPEC, ANY_SPEC, ANY_SPEC] + [ANY_SPEC] * BLOCKS,
        (ANY_SPEC, VMEM_SPEC),
        [
            pltpu.VMEM((BLOCKS, bonds, width, width), BF16),
            pltpu.VMEM((pairs, bonds, width, width), BF16),
            pltpu.VMEM((pairs, width, width), BF16),
            pltpu.VMEM((width, pairs, width), BF16),
            pltpu.VMEM((pairs, width, width), BF16),
            pltpu.VMEM((bonds, width, width), BF16),
            pltpu.VMEM((pairs, width, width), F32),
            pltpu.SemaphoreType.DMA((BLOCKS + 2,)),
            pltpu.SemaphoreType.DMA((2, pairs)),
            pltpu.SemaphoreType.DMA((pairs,)),
        ],
    )(charge, rank, psi, renv, mpo, x3_low, x3_high, *blocks)


def settle(total, mine, twin_stat, count):
    width = total.shape[1]
    return call(
        functools.partial(settle_kernel, count),
        "settle",
        10**4,
        (jax.ShapeDtypeStruct((2, width), F32), jax.ShapeDtypeStruct((8, width), F32)),
        [VMEM_SPEC] * 3,
        (VMEM_SPEC, VMEM_SPEC),
        [],
    )(total, mine, twin_stat)


def partner(value, bits):
    axes = ("seg", "sec")
    n = lax.axis_size(axes)
    return lax.ppermute(value, axes, [(i, i ^ bits) for i in range(n)])


def hop(value):
    n = lax.axis_size("sec")
    return lax.ppermute(value, "sec", [(i, (i + (2 if i % 2 == 0 else -2)) % n) for i in range(n)])


def cross_hop(value):
    n = lax.axis_size("sec")
    return lax.ppermute(value, "sec", [(i, (i + (-2 if i % 2 == 0 else 2)) % n ^ 1) for i in range(n)])


def twin(value):
    n = lax.axis_size("sec")
    return lax.ppermute(value, "sec", [(i, i ^ 1) for i in range(n)])


def from_behind(value):
    n = lax.axis_size("seg")
    return lax.ppermute(value, "seg", [(i, i + 1) for i in range(n - 1)])


def shards(psi, env_build, env_right, site_left, site_right, charge, rank):
    nsec = lax.axis_size("sec")
    sector = lax.axis_index("sec")
    segment = lax.axis_index("seg")
    x = psi[0, 0]
    renv = env_right[0, 0]
    pairs, width = x.shape[0], x.shape[2]
    count = float(nsec * pairs * width * width)

    env = env_build[0, 0]
    moved = from_behind(env)
    tall = (site_left.shape[0] * pairs, site_left.shape[1])
    ends = (site_left.transpose(0, 2, 3, 1).reshape(tall), site_right.transpose(0, 2, 3, 1).reshape(tall))
    x3_low, mpo = front(x, renv, *ends, 0, 2)
    moved, x3_low = lax.optimization_barrier((moved, x3_low))
    own = jnp.where(segment == 0, env, moved)

    o1 = hop(own)
    waited, x_then = lax.optimization_barrier((own, x))
    x3_high, _ = front(x_then, renv, *ends, 1, 2)
    waited, x3_high = lax.optimization_barrier((waited, x3_high))
    t1 = cross_hop(waited)
    o2 = hop(o1)
    t2 = hop(t1)
    o3 = hop(o2)
    t3 = hop(t2)
    o4 = hop(o3)
    blocks = [own, twin(own), o1, t1, o2, t2, o3, t3]
    blocks += [o4, twin(o4), twin(t3), twin(o3), twin(t2), twin(o2), twin(t1), twin(o1)]
    v, stat = back(charge, rank, x, renv, mpo, x3_low, x3_high, blocks)

    twin_stat = partner(stat, 1)
    total = stat + twin_stat
    for bits in (3, 5, 13):
        total = total + partner(total, bits)
    share, out = settle(total, stat, twin_stat, count)
    state = (v * out[0, 0]).astype(BF16)
    for bits in (1, 3, 4, 12):
        share = share + partner(share, nsec * bits + 1)
    wanted = (iota(share.shape, 0) == sector % 2) & (iota(share.shape, 1) <= segment)
    weight = jnp.sum(jnp.where(wanted, share, 0.0))
    return state[None, None], out[1:2, 0], weight.reshape(1, 1)


def solution(mesh):
    return jax.shard_map(
        shards,
        mesh=mesh,
        in_specs=(
            P("seg", "sec", None, None, None),
            P("seg", "sec", None, None, None),
            P("seg", "sec", None, None, None),
            P(),
            P(),
            P(),
            P("sec"),
        ),
        out_specs=(P("seg", "sec", None, None, None), P("seg"), P("seg", "sec")),
        check_vma=False,
    )
```

```python
import functools

import jax
import jax.numpy as jnp
from jax import lax
from jax.experimental import pallas as pl
from jax.experimental.pallas import tpu as pltpu
from jax.sharding import PartitionSpec as P

F32 = jnp.float32
BF16 = jnp.bfloat16


LOCAL = 4
BLOCKS = 16
FINISH = 4
VMEM_LIMIT = 60 * 2**20


def iota(shape, dim):
    return lax.broadcasted_iota(jnp.int32, shape, dim)


def pair_mpo(left_ref, right_ref):
    rows, bonds = left_ref.shape
    pairs = LOCAL * LOCAL
    wide = 256
    over_w = (iota((bonds, wide), 0) == iota((bonds, wide), 1) // pairs).astype(BF16)
    big = jnp.dot(right_ref[...], over_w, preferred_element_type=F32)
    same = (iota((rows, wide), 0) % pairs) == (iota((rows, wide), 1) % pairs)
    big = jnp.where(same, big, 0.0).astype(BF16)
    by_m = (iota((16, rows), 0) == iota((16, rows), 1) // pairs).astype(BF16)
    right = jnp.dot(by_m, big, preferred_element_type=F32).astype(BF16)
    joined = jnp.dot(left_ref[...], right[:bonds], preferred_element_type=F32)
    gap = iota((rows, wide), 0) % LOCAL - (iota((rows, wide), 1) // LOCAL) % LOCAL
    out = jnp.zeros((rows, wide), F32)
    for d in range(1 - LOCAL, LOCAL):
        moved = pltpu.roll(pltpu.roll(joined, d % rows, 0), (-LOCAL * d) % wide, 1)
        out = jnp.where(gap == d, moved, out)
    return out[:, :rows].astype(BF16)


def turn(src_ref, xt_ref):
    for j in range(src_ref.shape[1] // 16):
        xt_ref[j * 16 : (j + 1) * 16] = jnp.swapaxes(src_ref[:, j * 16 : (j + 1) * 16, :], 0, 1)


def spread(xt_ref, renv_ref, mpo, x3_ref, begin=0, done=None):
    states, pairs, width = xt_ref.shape
    bonds = renv_ref.shape[0]
    for at in range(begin, states, 16):
        xa = xt_ref[at : at + 16].reshape(16 * pairs, width)
        first = []
        for k in range(bonds // 2):
            both = jnp.concatenate([renv_ref[2 * k], renv_ref[2 * k + 1]], axis=1)
            got = jnp.dot(xa, both, preferred_element_type=F32).astype(BF16)
            first += [got[:, :width], got[:, width:]]
        rows = []
        for i in range(8):
            sides = []
            for a in (2 * i, 2 * i + 1):
                sides.append(jnp.concatenate([f[a * pairs : (a + 1) * pairs] for f in first], axis=0))
            out = jnp.dot(mpo, jnp.concatenate(sides, axis=1), preferred_element_type=F32).astype(BF16)
            rows += [out[:, :width], out[:, width:]]
        for l in range(bonds):
            block = jnp.stack([row[l * pairs : (l + 1) * pairs] for row in rows], axis=0)
            x3_ref[:, l, at : at + 16, :] = jnp.swapaxes(block, 0, 1)
        if done is not None:
            done(at)


def front_kernel(psi_any, renv_any, left_ref, right_ref, x3_any, mpo_ref, psi_ref, renv_ref, xt_ref, x3_ref, sem_ref, out_sem):
    copies = [
        pltpu.make_async_copy(psi_any.at[:, pl.ds(0, psi_ref.shape[1])], psi_ref, sem_ref.at[0]),
        pltpu.make_async_copy(renv_any, renv_ref, sem_ref.at[1]),
    ]
    for copy in copies:
        copy.start()
    mpo = pair_mpo(left_ref, right_ref)
    mpo_ref[...] = mpo
    for copy in copies:
        copy.wait()
    turn(psi_ref, xt_ref)
    sent = []

    def done(at):
        rows = pl.ds(at, 16)
        sent.append(pltpu.make_async_copy(x3_ref.at[:, :, rows], x3_any.at[:, :, rows], out_sem.at[at // 16]))
        sent[-1].start()

    spread(xt_ref, renv_ref, mpo, x3_ref, 0, done)
    for copy in sent:
        copy.wait()


def contract(lenv_ref, slot, x3_ref, q):
    bonds = lenv_ref.shape[1]
    total = None
    for k in range(bonds // 2):
        lhs = jnp.concatenate([lenv_ref[slot, 2 * k], lenv_ref[slot, 2 * k + 1]], axis=1)
        rhs = jnp.concatenate([x3_ref[q, 2 * k], x3_ref[q, 2 * k + 1]], axis=0)
        part = jnp.dot(lhs, rhs, preferred_element_type=F32)
        total = part if total is None else total + part
    return total


def slot_of(charge_ref, q):
    sector = lax.axis_index("sec")
    left = (sector - charge_ref[q]) & 15
    core = sector & 1
    ahead = (sector >> 1) - (left >> 1)
    hops = jnp.where(core == 0, ahead, -ahead) & 7
    return 2 * hops + ((left ^ sector) & 1)


def back_kernel(charge_ref, rank_ref, psi_any, renv_any, mpo_ref, x3_any, *rest):
    blocks = rest[:BLOCKS]
    v_any, stat_ref, lenv_ref, x3_ref, u_ref, xt_ref, psi_ref, renv_ref, v_ref = rest[BLOCKS:-3]
    sem_ref, x3_sem, v_sem = rest[-3:]
    pairs, width = psi_ref.shape[0], psi_ref.shape[2]
    done = x3_any.shape[2]
    first = [
        pltpu.make_async_copy(psi_any, psi_ref, sem_ref.at[BLOCKS]),
        pltpu.make_async_copy(renv_any, renv_ref, sem_ref.at[BLOCKS + 1]),
    ]
    second = [pltpu.make_async_copy(blocks[i], lenv_ref.at[i], sem_ref.at[i]) for i in range(BLOCKS)]
    second.append(pltpu.make_async_copy(x3_any, x3_ref.at[:, :, pl.ds(0, done)], x3_sem))
    for copy in first + second:
        copy.start()
    slots = [slot_of(charge_ref, q) for q in range(pairs)]
    keep = iota((width, width), 1) < rank_ref[0]
    zero = jnp.zeros((width, width), F32)
    for copy in first:
        copy.wait()
    turn(psi_ref, xt_ref)
    spread(xt_ref, renv_ref, mpo_ref[...], x3_ref, done)
    for copy in second:
        copy.wait()
    first_sq = zero
    for q in range(pairs):
        h = contract(lenv_ref, slots[q], x3_ref, q)
        u = jnp.where(keep, psi_ref[q].astype(F32) - 0.5 * h, 0.0)
        u_ref[q] = u.astype(BF16)
        first_sq = first_sq + u * u
    turn(u_ref, xt_ref)
    spread(xt_ref, renv_ref, mpo_ref[...], x3_ref)
    sq, inner, own = zero, zero, zero
    sent = []
    for q in range(pairs):
        h = contract(lenv_ref, slots[q], x3_ref, q)
        x = u_ref[q].astype(F32)
        v = jnp.where(keep, x - 0.5 * h, 0.0)
        v_ref[q] = v
        sent.append(pltpu.make_async_copy(v_ref.at[q], v_any.at[q], v_sem.at[q]))
        sent[-1].start()
        sq, inner, own = sq + v * v, inner + x * h, own + x * x
    for i, part in enumerate((first_sq, sq, inner, own)):
        stat_ref[i : i + 1] = jnp.sum(part, axis=0, keepdims=True)
    for copy in sent:
        copy.wait()


def settle_kernel(count, total_ref, mine_ref, twin_ref, share_ref, out_ref):
    width = total_ref.shape[1]
    first_sq, sq, inner, own = [jnp.sum(total_ref[i : i + 1], axis=1, keepdims=True) for i in range(4)]
    one = lax.rsqrt(first_sq / count + 1e-06)
    scale = one * lax.rsqrt(one * one * sq / count + 1e-06)
    out_ref[...] = jnp.where(iota((8, width), 0) == 0, scale, inner / own)
    mine = jnp.sum(mine_ref[1:2], axis=1, keepdims=True)
    twin = jnp.sum(twin_ref[1:2], axis=1, keepdims=True)
    row = iota((2, width), 0)
    here = jnp.where(row == (lax.axis_index("sec") & 1), mine, twin)
    share = jnp.log(float(lax.axis_size("sec")) * here / sq)
    share_ref[...] = jnp.where(iota((2, width), 1) == lax.axis_index("seg"), share, 0.0)


def finish_kernel(v_any, out_ref, state_any, v_ref, state_ref, in_sem, out_sem):
    pairs = v_ref.shape[0]
    part = pairs // FINISH
    loads, stores = [], []
    for i in range(FINISH):
        rows = pl.ds(i * part, part)
        loads.append(pltpu.make_async_copy(v_any.at[rows], v_ref.at[rows], in_sem.at[i]))
        stores.append(pltpu.make_async_copy(state_ref.at[rows], state_any.at[rows], out_sem.at[i]))
        loads[i].start()
    scale = out_ref[0:1, :]
    for i in range(FINISH):
        loads[i].wait()
        for q in range(i * part, (i + 1) * part):
            state_ref[q] = (v_ref[q] * scale).astype(BF16)
        stores[i].start()
    for store in stores:
        store.wait()


VMEM_SPEC = pl.BlockSpec(memory_space=pltpu.VMEM)
SMEM_SPEC = pl.BlockSpec(memory_space=pltpu.SMEM)
ANY_SPEC = pl.BlockSpec(memory_space=pl.ANY)


def call(kernel, name, flops, out_shape, in_specs, out_specs, scratch):
    return pl.pallas_call(
        kernel,
        out_shape=out_shape,
        in_specs=in_specs,
        out_specs=out_specs,
        scratch_shapes=scratch,
        compiler_params=pltpu.CompilerParams(vmem_limit_bytes=VMEM_LIMIT),
        cost_estimate=pl.CostEstimate(flops=flops, bytes_accessed=8 * 10**6, transcendentals=0),
        name=name,
    )


def front(psi, renv, left, right, states):
    pairs, width = psi.shape[0], psi.shape[2]
    bonds = renv.shape[0]
    rows = bonds * pairs
    return call(
        front_kernel,
        "front",
        5 * 10**8,
        (jax.ShapeDtypeStruct((pairs, bonds, states, width), BF16), jax.ShapeDtypeStruct((rows, rows), BF16)),
        [ANY_SPEC, ANY_SPEC, VMEM_SPEC, VMEM_SPEC],
        (ANY_SPEC, VMEM_SPEC),
        [
            pltpu.VMEM((pairs, states, width), BF16),
            pltpu.VMEM((bonds, width, width), BF16),
            pltpu.VMEM((states, pairs, width), BF16),
            pltpu.VMEM((pairs, bonds, states, width), BF16),
            pltpu.SemaphoreType.DMA((2,)),
            pltpu.SemaphoreType.DMA((states // 16,)),
        ],
    )(psi, renv, left, right)


def back(charge, rank, psi, renv, mpo, x3, blocks):
    pairs, width = psi.shape[0], psi.shape[2]
    bonds = renv.shape[0]
    return call(
        back_kernel,
        "back",
        4 * 10**9,
        (jax.ShapeDtypeStruct((pairs, width, width), F32), jax.ShapeDtypeStruct((4, width), F32)),
        [SMEM_SPEC, SMEM_SPEC, ANY_SPEC, ANY_SPEC, VMEM_SPEC, ANY_SPEC] + [ANY_SPEC] * BLOCKS,
        (ANY_SPEC, VMEM_SPEC),
        [
            pltpu.VMEM((BLOCKS, bonds, width, width), BF16),
            pltpu.VMEM((pairs, bonds, width, width), BF16),
            pltpu.VMEM((pairs, width, width), BF16),
            pltpu.VMEM((width, pairs, width), BF16),
            pltpu.VMEM((pairs, width, width), BF16),
            pltpu.VMEM((bonds, width, width), BF16),
            pltpu.VMEM((pairs, width, width), F32),
            pltpu.SemaphoreType.DMA((BLOCKS + 2,)),
            pltpu.SemaphoreType.DMA,
            pltpu.SemaphoreType.DMA((pairs,)),
        ],
    )(charge, rank, psi, renv, mpo, x3, *blocks)


def settle(total, mine, twin_stat, count):
    width = total.shape[1]
    return call(
        functools.partial(settle_kernel, count),
        "settle",
        10**4,
        (jax.ShapeDtypeStruct((2, width), F32), jax.ShapeDtypeStruct((8, width), F32)),
        [VMEM_SPEC] * 3,
        (VMEM_SPEC, VMEM_SPEC),
        [],
    )(total, mine, twin_stat)


def finish(v, out):
    return call(
        finish_kernel,
        "finish",
        10**6,
        jax.ShapeDtypeStruct(v.shape, BF16),
        [ANY_SPEC, VMEM_SPEC],
        ANY_SPEC,
        [
            pltpu.VMEM(v.shape, F32),
            pltpu.VMEM(v.shape, BF16),
            pltpu.SemaphoreType.DMA((FINISH,)),
            pltpu.SemaphoreType.DMA((FINISH,)),
        ],
    )(v, out)


def partner(value, bits):
    axes = ("seg", "sec")
    n = lax.axis_size(axes)
    return lax.ppermute(value, axes, [(i, i ^ bits) for i in range(n)])


def hop(value):
    n = lax.axis_size("sec")
    return lax.ppermute(value, "sec", [(i, (i + (2 if i % 2 == 0 else -2)) % n) for i in range(n)])


def cross_hop(value):
    n = lax.axis_size("sec")
    return lax.ppermute(value, "sec", [(i, (i + (-2 if i % 2 == 0 else 2)) % n ^ 1) for i in range(n)])


def twin(value):
    n = lax.axis_size("sec")
    return lax.ppermute(value, "sec", [(i, i ^ 1) for i in range(n)])


def from_behind(value):
    n = lax.axis_size("seg")
    return lax.ppermute(value, "seg", [(i, i + 1) for i in range(n - 1)])


def shards(psi, env_build, env_right, site_left, site_right, charge, rank):
    nsec = lax.axis_size("sec")
    sector = lax.axis_index("sec")
    segment = lax.axis_index("seg")
    x = psi[0, 0]
    renv = env_right[0, 0]
    pairs, width = x.shape[0], x.shape[2]
    count = float(nsec * pairs * width * width)

    env = env_build[0, 0]
    moved = from_behind(env)
    tall = (site_left.shape[0] * pairs, site_left.shape[1])
    ends = (site_left.transpose(0, 2, 3, 1).reshape(tall), site_right.transpose(0, 2, 3, 1).reshape(tall))
    own = jnp.where(segment == 0, env, moved)

    o1 = hop(own)
    waited, x_then = lax.optimization_barrier((own, x))
    x3, mpo = front(x_then, renv, *ends, width // 4)
    waited, x3 = lax.optimization_barrier((waited, x3))
    t1 = cross_hop(waited)
    o2 = hop(o1)
    t2 = hop(t1)
    o3 = hop(o2)
    t3 = hop(t2)
    o4 = hop(o3)
    blocks = [own, twin(own), o1, t1, o2, t2, o3, t3]
    blocks += [o4, twin(o4), twin(t3), twin(o3), twin(t2), twin(o2), twin(t1), twin(o1)]
    v, stat = back(charge, rank, x, renv, mpo, x3, blocks)

    twin_stat = partner(stat, 1)
    total = stat + twin_stat
    for bits in (3, 5, 13):
        total = total + partner(total, bits)
    share, out = settle(total, stat, twin_stat, count)
    state = finish(v, out)
    for bits in (1, 3, 4, 12):
        share = share + partner(share, nsec * bits + 1)
        if bits == 1:
            share, state = lax.optimization_barrier((share, state))
    wanted = (iota(share.shape, 0) == sector % 2) & (iota(share.shape, 1) <= segment)
    weight = jnp.sum(jnp.where(wanted, share, 0.0))
    return state[None, None], out[1:2, 0], weight.reshape(1, 1)


def solution(mesh):
    return jax.shard_map(
        shards,
        mesh=mesh,
        in_specs=(
            P("seg", "sec", None, None, None),
            P("seg", "sec", None, None, None),
            P("seg", "sec", None, None, None),
            P(),
            P(),
            P(),
            P("sec"),
        ),
        out_specs=(P("seg", "sec", None, None, None), P("seg"), P("seg", "sec")),
        check_vma=False,
    )
```

```python
import functools

import jax
import jax.numpy as jnp
from jax import lax
from jax.experimental import pallas as pl
from jax.experimental.pallas import tpu as pltpu
from jax.sharding import PartitionSpec as P

F32 = jnp.float32
BF16 = jnp.bfloat16


LOCAL = 4
BLOCKS = 16
CHUNK = 32
FINISH = 4
LATEST = (9, 10)
VMEM_LIMIT = 60 * 2**20


def iota(shape, dim):
    return lax.broadcasted_iota(jnp.int32, shape, dim)


def pair_mpo(left_ref, right_ref):
    rows, bonds = left_ref.shape
    pairs = LOCAL * LOCAL
    wide = 256
    over_w = (iota((bonds, wide), 0) == iota((bonds, wide), 1) // pairs).astype(BF16)
    big = jnp.dot(right_ref[...], over_w, preferred_element_type=F32)
    same = (iota((rows, wide), 0) % pairs) == (iota((rows, wide), 1) % pairs)
    big = jnp.where(same, big, 0.0).astype(BF16)
    by_m = (iota((16, rows), 0) == iota((16, rows), 1) // pairs).astype(BF16)
    right = jnp.dot(by_m, big, preferred_element_type=F32).astype(BF16)
    joined = jnp.dot(left_ref[...], right[:bonds], preferred_element_type=F32)
    gap = iota((rows, wide), 0) % LOCAL - (iota((rows, wide), 1) // LOCAL) % LOCAL
    out = jnp.zeros((rows, wide), F32)
    for d in range(1 - LOCAL, LOCAL):
        moved = pltpu.roll(pltpu.roll(joined, d % rows, 0), (-LOCAL * d) % wide, 1)
        out = jnp.where(gap == d, moved, out)
    return out[:, :rows].astype(BF16)


def turn(src_ref, xt_ref):
    for j in range(src_ref.shape[1] // 16):
        xt_ref[j * 16 : (j + 1) * 16] = jnp.swapaxes(src_ref[:, j * 16 : (j + 1) * 16, :], 0, 1)


def spread(xt_ref, renv_ref, mpo, x3_ref, begin=0, done=None):
    states, pairs, width = xt_ref.shape
    bonds = renv_ref.shape[0]
    beside = jnp.concatenate([renv_ref[w] for w in range(bonds)], axis=1)
    for start in range(begin, states, CHUNK):
        xa = xt_ref[start : start + CHUNK].reshape(CHUNK * pairs, width)
        first = jnp.dot(xa, beside, preferred_element_type=F32).astype(BF16)
        for at in range(0, CHUNK, 16):
            rows = []
            for i in range(at, at + 16, 2):
                sides = []
                for a in (i, i + 1):
                    row = first[a * pairs : (a + 1) * pairs]
                    sides.append(jnp.concatenate([row[:, w * width : (w + 1) * width] for w in range(bonds)], axis=0))
                out = jnp.dot(mpo, jnp.concatenate(sides, axis=1), preferred_element_type=F32).astype(BF16)
                rows += [out[:, :width], out[:, width:]]
            for l in range(bonds):
                block = jnp.stack([row[l * pairs : (l + 1) * pairs] for row in rows], axis=0)
                x3_ref[:, l, start + at : start + at + 16, :] = jnp.swapaxes(block, 0, 1)
        if done is not None:
            done(start)


def operators_kernel(left_ref, right_ref, mpo_ref):
    mpo_ref[...] = pair_mpo(left_ref, right_ref)


def front_kernel(psi_any, renv_any, left_ref, right_ref, x3_any, psi_ref, renv_ref, xt_ref, x3_ref, sem_ref, out_sem):
    copies = [
        pltpu.make_async_copy(psi_any.at[:, pl.ds(0, psi_ref.shape[1])], psi_ref, sem_ref.at[0]),
        pltpu.make_async_copy(renv_any, renv_ref, sem_ref.at[1]),
    ]
    for copy in copies:
        copy.start()
    mpo = pair_mpo(left_ref, right_ref)
    for copy in copies:
        copy.wait()
    turn(psi_ref, xt_ref)
    sent = []

    def done(at):
        rows = pl.ds(at, CHUNK)
        sent.append(pltpu.make_async_copy(x3_ref.at[:, :, rows], x3_any.at[:, :, rows], out_sem.at[at // CHUNK]))
        sent[-1].start()

    spread(xt_ref, renv_ref, mpo, x3_ref, 0, done)
    for copy in sent:
        copy.wait()


def contract(lenv_ref, slot, x3_ref, q):
    bonds = lenv_ref.shape[1]
    lhs = jnp.concatenate([lenv_ref[slot, l] for l in range(bonds)], axis=1)
    rhs = jnp.concatenate([x3_ref[q, l] for l in range(bonds)], axis=0)
    return jnp.dot(lhs, rhs, preferred_element_type=F32)


def folded(value):
    return jnp.sum(value.reshape(value.shape[0] // 8, 8, value.shape[1]), axis=0)


def slot_of(charge_ref, q):
    sector = lax.axis_index("sec")
    left = (sector - charge_ref[q]) & 15
    core = sector & 1
    ahead = (sector >> 1) - (left >> 1)
    hops = jnp.where(core == 0, ahead, -ahead) & 7
    return 2 * hops + ((left ^ sector) & 1)


def back_kernel(charge_ref, rank_ref, psi_any, renv_any, mpo_ref, x3_any, *rest):
    blocks = rest[:BLOCKS]
    v_any, stat_ref, lenv_ref, x3_ref, u_ref, xt_ref, psi_ref, renv_ref, v_ref = rest[BLOCKS:-3]
    sem_ref, x3_sem, v_sem = rest[-3:]
    pairs, width = psi_ref.shape[0], psi_ref.shape[2]
    done = x3_any.shape[2]
    first = [
        pltpu.make_async_copy(psi_any, psi_ref, sem_ref.at[BLOCKS]),
        pltpu.make_async_copy(renv_any, renv_ref, sem_ref.at[BLOCKS + 1]),
    ]
    second = [pltpu.make_async_copy(blocks[i], lenv_ref.at[i], sem_ref.at[i]) for i in range(BLOCKS)]
    second.append(pltpu.make_async_copy(x3_any, x3_ref.at[:, :, pl.ds(0, done)], x3_sem))
    for copy in first + second:
        copy.start()
    slots = [slot_of(charge_ref, q) for q in range(pairs)]
    keep = iota((width, width), 1) < rank_ref[0]
    zero = jnp.zeros((8, width), F32)
    for copy in first:
        copy.wait()
    turn(psi_ref, xt_ref)
    spread(xt_ref, renv_ref, mpo_ref[...], x3_ref, done)
    for copy in second:
        copy.wait()
    first_sq = zero
    for q in range(pairs):
        h = contract(lenv_ref, slots[q], x3_ref, q)
        u = jnp.where(keep, psi_ref[q].astype(F32) - 0.5 * h, 0.0)
        u_ref[q] = u.astype(BF16)
        first_sq = first_sq + folded(u * u)
    turn(u_ref, xt_ref)
    spread(xt_ref, renv_ref, mpo_ref[...], x3_ref)
    sq, inner, own = zero, zero, zero
    sent = []
    for q in range(pairs):
        h = contract(lenv_ref, slots[q], x3_ref, q)
        x = u_ref[q].astype(F32)
        v = jnp.where(keep, x - 0.5 * h, 0.0)
        v_ref[q] = v
        sent.append(pltpu.make_async_copy(v_ref.at[q], v_any.at[q], v_sem.at[q]))
        sent[-1].start()
        sq, inner, own = sq + folded(v * v), inner + folded(x * h), own + folded(x * x)
    for i, part in enumerate((first_sq, sq, inner, own)):
        stat_ref[i : i + 1] = jnp.sum(part, axis=0, keepdims=True)
    for copy in sent:
        copy.wait()


def settle_kernel(count, half_ref, other_ref, mine_ref, twin_ref, share_ref, out_ref):
    width = half_ref.shape[1]
    total = jnp.sum(half_ref[...] + other_ref[...], axis=1, keepdims=True)
    first_sq, sq, inner, own = [total[i : i + 1] for i in range(4)]
    one = lax.rsqrt(first_sq / count + 1e-06)
    scale = one * lax.rsqrt(one * one * sq / count + 1e-06)
    out_ref[...] = jnp.where(iota((8, width), 0) == 0, scale, inner / own)
    mine = jnp.sum(mine_ref[1:2], axis=1, keepdims=True)
    twin = jnp.sum(twin_ref[1:2], axis=1, keepdims=True)
    row = iota((2, width), 0)
    here = jnp.where(row == (lax.axis_index("sec") & 1), mine, twin)
    share = jnp.log(float(lax.axis_size("sec")) * here / sq)
    share_ref[...] = jnp.where(iota((2, width), 1) == lax.axis_index("seg"), share, 0.0)


def finish_kernel(v_any, out_ref, state_any, v_ref, state_ref, in_sem, out_sem):
    pairs = v_ref.shape[0]
    part = pairs // FINISH
    loads, stores = [], []
    for i in range(FINISH):
        rows = pl.ds(i * part, part)
        loads.append(pltpu.make_async_copy(v_any.at[rows], v_ref.at[rows], in_sem.at[i]))
        stores.append(pltpu.make_async_copy(state_ref.at[rows], state_any.at[rows], out_sem.at[i]))
        loads[i].start()
    scale = out_ref[0:1, :]
    for i in range(FINISH):
        loads[i].wait()
        for q in range(i * part, (i + 1) * part):
            state_ref[q] = (v_ref[q] * scale).astype(BF16)
        stores[i].start()
    for store in stores:
        store.wait()


VMEM_SPEC = pl.BlockSpec(memory_space=pltpu.VMEM)
SMEM_SPEC = pl.BlockSpec(memory_space=pltpu.SMEM)
ANY_SPEC = pl.BlockSpec(memory_space=pl.ANY)


def call(kernel, name, flops, out_shape, in_specs, out_specs, scratch):
    return pl.pallas_call(
        kernel,
        out_shape=out_shape,
        in_specs=in_specs,
        out_specs=out_specs,
        scratch_shapes=scratch,
        compiler_params=pltpu.CompilerParams(vmem_limit_bytes=VMEM_LIMIT),
        cost_estimate=pl.CostEstimate(flops=flops, bytes_accessed=8 * 10**6, transcendentals=0),
        name=name,
    )


def operators(left, right):
    rows = left.shape[0]
    return call(
        operators_kernel,
        "operators",
        10**8,
        jax.ShapeDtypeStruct((rows, rows), BF16),
        [VMEM_SPEC, VMEM_SPEC],
        VMEM_SPEC,
        [],
    )(left, right)


def front(psi, renv, left, right, states):
    pairs, width = psi.shape[0], psi.shape[2]
    bonds = renv.shape[0]
    return call(
        front_kernel,
        "front",
        5 * 10**8,
        jax.ShapeDtypeStruct((pairs, bonds, states, width), BF16),
        [ANY_SPEC, ANY_SPEC, VMEM_SPEC, VMEM_SPEC],
        ANY_SPEC,
        [
            pltpu.VMEM((pairs, states, width), BF16),
            pltpu.VMEM((bonds, width, width), BF16),
            pltpu.VMEM((states, pairs, width), BF16),
            pltpu.VMEM((pairs, bonds, states, width), BF16),
            pltpu.SemaphoreType.DMA((2,)),
            pltpu.SemaphoreType.DMA((states // CHUNK,)),
        ],
    )(psi, renv, left, right)


def back(charge, rank, psi, renv, mpo, x3, blocks):
    pairs, width = psi.shape[0], psi.shape[2]
    bonds = renv.shape[0]
    return call(
        back_kernel,
        "back",
        4 * 10**9,
        (jax.ShapeDtypeStruct((pairs, width, width), F32), jax.ShapeDtypeStruct((4, width), F32)),
        [SMEM_SPEC, SMEM_SPEC, ANY_SPEC, ANY_SPEC, VMEM_SPEC, ANY_SPEC]
        + [VMEM_SPEC if i in LATEST else ANY_SPEC for i in range(BLOCKS)],
        (ANY_SPEC, VMEM_SPEC),
        [
            pltpu.VMEM((BLOCKS, bonds, width, width), BF16),
            pltpu.VMEM((pairs, bonds, width, width), BF16),
            pltpu.VMEM((pairs, width, width), BF16),
            pltpu.VMEM((width, pairs, width), BF16),
            pltpu.VMEM((pairs, width, width), BF16),
            pltpu.VMEM((bonds, width, width), BF16),
            pltpu.VMEM((pairs, width, width), F32),
            pltpu.SemaphoreType.DMA((BLOCKS + 2,)),
            pltpu.SemaphoreType.DMA,
            pltpu.SemaphoreType.DMA((pairs,)),
        ],
    )(charge, rank, psi, renv, mpo, x3, *blocks)


def settle(half, other, mine, twin_stat, count):
    width = half.shape[1]
    return call(
        functools.partial(settle_kernel, count),
        "settle",
        10**4,
        (jax.ShapeDtypeStruct((2, width), F32), jax.ShapeDtypeStruct((8, width), F32)),
        [VMEM_SPEC] * 4,
        (VMEM_SPEC, VMEM_SPEC),
        [],
    )(half, other, mine, twin_stat)


def finish(v, out):
    return call(
        finish_kernel,
        "finish",
        10**6,
        jax.ShapeDtypeStruct(v.shape, BF16),
        [ANY_SPEC, VMEM_SPEC],
        ANY_SPEC,
        [
            pltpu.VMEM(v.shape, F32),
            pltpu.VMEM(v.shape, BF16),
            pltpu.SemaphoreType.DMA((FINISH,)),
            pltpu.SemaphoreType.DMA((FINISH,)),
        ],
    )(v, out)


def partner(value, bits):
    axes = ("seg", "sec")
    n = lax.axis_size(axes)
    return lax.ppermute(value, axes, [(i, i ^ bits) for i in range(n)])


def hop(value):
    n = lax.axis_size("sec")
    return lax.ppermute(value, "sec", [(i, (i + (2 if i % 2 == 0 else -2)) % n) for i in range(n)])


def cross_hop(value):
    n = lax.axis_size("sec")
    return lax.ppermute(value, "sec", [(i, (i + (-2 if i % 2 == 0 else 2)) % n ^ 1) for i in range(n)])


def twin(value):
    n = lax.axis_size("sec")
    return lax.ppermute(value, "sec", [(i, i ^ 1) for i in range(n)])


def from_behind(value):
    n = lax.axis_size("seg")
    return lax.ppermute(value, "seg", [(i, i + 1) for i in range(n - 1)])


def shards(psi, env_build, env_right, site_left, site_right, charge, rank):
    nsec = lax.axis_size("sec")
    sector = lax.axis_index("sec")
    segment = lax.axis_index("seg")
    x = psi[0, 0]
    renv = env_right[0, 0]
    pairs, width = x.shape[0], x.shape[2]
    count = float(nsec * pairs * width * width)

    env = env_build[0, 0]
    moved = from_behind(env)
    tall = (site_left.shape[0] * pairs, site_left.shape[1])
    ends = (site_left.transpose(0, 2, 3, 1).reshape(tall), site_right.transpose(0, 2, 3, 1).reshape(tall))
    x3 = front(x, renv, *ends, width // 4)
    moved, x3 = lax.optimization_barrier((moved, x3))
    own = jnp.where(segment == 0, env, moved)

    o1 = hop(own)
    waited, ends = lax.optimization_barrier((own, ends))
    mpo = operators(*ends)
    waited, mpo = lax.optimization_barrier((waited, mpo))
    t1 = cross_hop(waited)
    o2 = hop(o1)
    t2 = hop(t1)
    o3 = hop(o2)
    t3 = hop(t2)
    o4 = hop(o3)
    blocks = [own, twin(own), o1, t1, o2, t2, o3, t3]
    blocks += [o4, twin(o4), twin(t3), twin(o3), twin(t2), twin(o2), twin(t1), twin(o1)]
    v, stat = back(charge, rank, x, renv, mpo, x3, blocks)

    twin_stat = partner(stat, 1)
    total = stat + twin_stat
    for bits in (3, 5):
        total = total + partner(total, bits)
    share, out = settle(total, partner(total, 13), stat, twin_stat, count)
    state = finish(v, out)
    for bits in (1, 3, 4, 12):
        share = share + partner(share, nsec * bits + 1)
        if bits == 1:
            share, state = lax.optimization_barrier((share, state))
    wanted = (iota(share.shape, 0) == sector % 2) & (iota(share.shape, 1) <= segment)
    weight = jnp.sum(jnp.where(wanted, share, 0.0))
    return state[None, None], out[1:2, 0], weight.reshape(1, 1)


def solution(mesh):
    return jax.shard_map(
        shards,
        mesh=mesh,
        in_specs=(
            P("seg", "sec", None, None, None),
            P("seg", "sec", None, None, None),
            P("seg", "sec", None, None, None),
            P(),
            P(),
            P(),
            P("sec"),
        ),
        out_specs=(P("seg", "sec", None, None, None), P("seg"), P("seg", "sec")),
        check_vma=False,
    )
```

```python
import functools

import jax
import jax.numpy as jnp
from jax import lax
from jax.experimental import pallas as pl
from jax.experimental.pallas import tpu as pltpu
from jax.sharding import PartitionSpec as P

F32 = jnp.float32
BF16 = jnp.bfloat16


LOCAL = 4
BLOCKS = 16
CHUNK = 32
FINISH = 4
VMEM_LIMIT = 40 * 2**20


def iota(shape, dim):
    return lax.broadcasted_iota(jnp.int32, shape, dim)


def pair_mpo(left_ref, right_ref):
    rows, bonds = left_ref.shape
    pairs = LOCAL * LOCAL
    wide = 256
    over_w = (iota((bonds, wide), 0) == iota((bonds, wide), 1) // pairs).astype(BF16)
    big = jnp.dot(right_ref[...], over_w, preferred_element_type=F32)
    same = (iota((rows, wide), 0) % pairs) == (iota((rows, wide), 1) % pairs)
    big = jnp.where(same, big, 0.0).astype(BF16)
    by_m = (iota((16, rows), 0) == iota((16, rows), 1) // pairs).astype(BF16)
    right = jnp.dot(by_m, big, preferred_element_type=F32).astype(BF16)
    joined = jnp.dot(left_ref[...], right[:bonds], preferred_element_type=F32)
    gap = iota((rows, wide), 0) % LOCAL - (iota((rows, wide), 1) // LOCAL) % LOCAL
    out = jnp.zeros((rows, wide), F32)
    for d in range(1 - LOCAL, LOCAL):
        moved = pltpu.roll(pltpu.roll(joined, d % rows, 0), (-LOCAL * d) % wide, 1)
        out = jnp.where(gap == d, moved, out)
    return out[:, :rows].astype(BF16)


def turn(src_ref, xt_ref):
    for j in range(src_ref.shape[1] // 16):
        xt_ref[j * 16 : (j + 1) * 16] = jnp.swapaxes(src_ref[:, j * 16 : (j + 1) * 16, :], 0, 1)


def spread(xt_ref, renv_ref, mpo, x3_ref, begin=0, done=None):
    states, pairs, width = xt_ref.shape
    bonds = renv_ref.shape[0]
    beside = jnp.concatenate([renv_ref[w] for w in range(bonds)], axis=1)
    for start in range(begin, states, CHUNK):
        xa = xt_ref[start : start + CHUNK].reshape(CHUNK * pairs, width)
        first = jnp.dot(xa, beside, preferred_element_type=F32).astype(BF16)
        for at in range(0, CHUNK, 16):
            rows = []
            for i in range(at, at + 16, 2):
                sides = []
                for a in (i, i + 1):
                    row = first[a * pairs : (a + 1) * pairs]
                    sides.append(jnp.concatenate([row[:, w * width : (w + 1) * width] for w in range(bonds)], axis=0))
                out = jnp.dot(mpo, jnp.concatenate(sides, axis=1), preferred_element_type=F32).astype(BF16)
                rows += [out[:, :width], out[:, width:]]
            for l in range(bonds):
                block = jnp.stack([row[l * pairs : (l + 1) * pairs] for row in rows], axis=0)
                x3_ref[:, l, start + at : start + at + 16, :] = jnp.swapaxes(block, 0, 1)
        if done is not None:
            done(start)


def operators_kernel(left_ref, right_ref, mpo_ref):
    mpo_ref[...] = pair_mpo(left_ref, right_ref)


def front_kernel(psi_any, renv_any, left_ref, right_ref, x3_any, psi_ref, renv_ref, xt_ref, x3_ref, sem_ref, out_sem):
    copies = [
        pltpu.make_async_copy(psi_any.at[:, pl.ds(0, psi_ref.shape[1])], psi_ref, sem_ref.at[0]),
        pltpu.make_async_copy(renv_any, renv_ref, sem_ref.at[1]),
    ]
    for copy in copies:
        copy.start()
    mpo = pair_mpo(left_ref, right_ref)
    for copy in copies:
        copy.wait()
    turn(psi_ref, xt_ref)
    sent = []

    def done(at):
        rows = pl.ds(at, CHUNK)
        sent.append(pltpu.make_async_copy(x3_ref.at[:, :, rows], x3_any.at[:, :, rows], out_sem.at[at // CHUNK]))
        sent[-1].start()

    spread(xt_ref, renv_ref, mpo, x3_ref, 0, done)
    for copy in sent:
        copy.wait()


def contract(lenv_ref, slot, x3_ref, q):
    bonds = lenv_ref.shape[1]
    lhs = jnp.concatenate([lenv_ref[slot, l] for l in range(bonds)], axis=1)
    rhs = jnp.concatenate([x3_ref[q, l] for l in range(bonds)], axis=0)
    return jnp.dot(lhs, rhs, preferred_element_type=F32)


def folded(value):
    return jnp.sum(value.reshape(value.shape[0] // 8, 8, value.shape[1]), axis=0)


def slot_of(charge_ref, q):
    sector = lax.axis_index("sec")
    left = (sector - charge_ref[q]) & 15
    core = sector & 1
    ahead = (sector >> 1) - (left >> 1)
    hops = jnp.where(core == 0, ahead, -ahead) & 7
    return 2 * hops + ((left ^ sector) & 1)


def back_kernel(charge_ref, rank_ref, psi_any, renv_any, mpo_ref, x3_any, *rest):
    blocks = rest[:BLOCKS]
    v_any, stat_ref, lenv_ref, x3_ref, u_ref, xt_ref, psi_ref, renv_ref, v_ref = rest[BLOCKS:-3]
    sem_ref, x3_sem, v_sem = rest[-3:]
    pairs, width = psi_ref.shape[0], psi_ref.shape[2]
    done = x3_any.shape[2]
    first = [
        pltpu.make_async_copy(psi_any, psi_ref, sem_ref.at[BLOCKS]),
        pltpu.make_async_copy(renv_any, renv_ref, sem_ref.at[BLOCKS + 1]),
    ]
    second = [pltpu.make_async_copy(blocks[i], lenv_ref.at[i], sem_ref.at[i]) for i in range(BLOCKS)]
    second.append(pltpu.make_async_copy(x3_any, x3_ref.at[:, :, pl.ds(0, done)], x3_sem))
    for copy in first + second:
        copy.start()
    slots = [slot_of(charge_ref, q) for q in range(pairs)]
    keep = iota((width, width), 1) < rank_ref[0]
    zero = jnp.zeros((8, width), F32)
    for copy in first:
        copy.wait()
    turn(psi_ref, xt_ref)
    spread(xt_ref, renv_ref, mpo_ref[...], x3_ref, done)
    for copy in second:
        copy.wait()
    first_sq = zero
    for q in range(pairs):
        h = contract(lenv_ref, slots[q], x3_ref, q)
        u = jnp.where(keep, psi_ref[q].astype(F32) - 0.5 * h, 0.0)
        u_ref[q] = u.astype(BF16)
        first_sq = first_sq + folded(u * u)
    turn(u_ref, xt_ref)
    spread(xt_ref, renv_ref, mpo_ref[...], x3_ref)
    sq, inner, own = zero, zero, zero
    sent = []
    for q in range(pairs):
        h = contract(lenv_ref, slots[q], x3_ref, q)
        x = u_ref[q].astype(F32)
        v = jnp.where(keep, x - 0.5 * h, 0.0)
        v_ref[q] = v
        sent.append(pltpu.make_async_copy(v_ref.at[q], v_any.at[q], v_sem.at[q]))
        sent[-1].start()
        sq, inner, own = sq + folded(v * v), inner + folded(x * h), own + folded(x * x)
    for i, part in enumerate((first_sq, sq, inner, own)):
        stat_ref[i : i + 1] = jnp.sum(part, axis=0, keepdims=True)
    for copy in sent:
        copy.wait()


def settle_kernel(count, half_ref, other_ref, mine_ref, twin_ref, share_ref, out_ref):
    width = half_ref.shape[1]
    total = jnp.sum(half_ref[...] + other_ref[...], axis=1, keepdims=True)
    first_sq, sq, inner, own = [total[i : i + 1] for i in range(4)]
    one = lax.rsqrt(first_sq / count + 1e-06)
    scale = one * lax.rsqrt(one * one * sq / count + 1e-06)
    out_ref[...] = jnp.where(iota((8, width), 0) == 0, scale, inner / own)
    mine = jnp.sum(mine_ref[1:2], axis=1, keepdims=True)
    twin = jnp.sum(twin_ref[1:2], axis=1, keepdims=True)
    row = iota((2, width), 0)
    here = jnp.where(row == (lax.axis_index("sec") & 1), mine, twin)
    share = jnp.log(float(lax.axis_size("sec")) * here / sq)
    share_ref[...] = jnp.where(iota((2, width), 1) == lax.axis_index("seg"), share, 0.0)


def finish_kernel(v_any, out_ref, state_any, v_ref, state_ref, in_sem, out_sem):
    pairs = v_ref.shape[0]
    part = pairs // FINISH
    loads, stores = [], []
    for i in range(FINISH):
        rows = pl.ds(i * part, part)
        loads.append(pltpu.make_async_copy(v_any.at[rows], v_ref.at[rows], in_sem.at[i]))
        stores.append(pltpu.make_async_copy(state_ref.at[rows], state_any.at[rows], out_sem.at[i]))
        loads[i].start()
    scale = out_ref[0:1, :]
    for i in range(FINISH):
        loads[i].wait()
        for q in range(i * part, (i + 1) * part):
            state_ref[q] = (v_ref[q] * scale).astype(BF16)
        stores[i].start()
    for store in stores:
        store.wait()


VMEM_SPEC = pl.BlockSpec(memory_space=pltpu.VMEM)
SMEM_SPEC = pl.BlockSpec(memory_space=pltpu.SMEM)
ANY_SPEC = pl.BlockSpec(memory_space=pl.ANY)


def call(kernel, name, flops, out_shape, in_specs, out_specs, scratch):
    return pl.pallas_call(
        kernel,
        out_shape=out_shape,
        in_specs=in_specs,
        out_specs=out_specs,
        scratch_shapes=scratch,
        compiler_params=pltpu.CompilerParams(vmem_limit_bytes=VMEM_LIMIT),
        cost_estimate=pl.CostEstimate(flops=flops, bytes_accessed=8 * 10**6, transcendentals=0),
        name=name,
    )


def operators(left, right):
    rows = left.shape[0]
    return call(
        operators_kernel,
        "operators",
        10**8,
        jax.ShapeDtypeStruct((rows, rows), BF16),
        [VMEM_SPEC, VMEM_SPEC],
        VMEM_SPEC,
        [],
    )(left, right)


def front(psi, renv, left, right, states):
    pairs, width = psi.shape[0], psi.shape[2]
    bonds = renv.shape[0]
    return call(
        front_kernel,
        "front",
        5 * 10**8,
        jax.ShapeDtypeStruct((pairs, bonds, states, width), BF16),
        [ANY_SPEC, ANY_SPEC, VMEM_SPEC, VMEM_SPEC],
        ANY_SPEC,
        [
            pltpu.VMEM((pairs, states, width), BF16),
            pltpu.VMEM((bonds, width, width), BF16),
            pltpu.VMEM((states, pairs, width), BF16),
            pltpu.VMEM((pairs, bonds, states, width), BF16),
            pltpu.SemaphoreType.DMA((2,)),
            pltpu.SemaphoreType.DMA((states // CHUNK,)),
        ],
    )(psi, renv, left, right)


def back(charge, rank, psi, renv, mpo, x3, blocks):
    pairs, width = psi.shape[0], psi.shape[2]
    bonds = renv.shape[0]
    return call(
        back_kernel,
        "back",
        4 * 10**9,
        (jax.ShapeDtypeStruct((pairs, width, width), F32), jax.ShapeDtypeStruct((4, width), F32)),
        [SMEM_SPEC, SMEM_SPEC, ANY_SPEC, ANY_SPEC, VMEM_SPEC, ANY_SPEC] + [ANY_SPEC] * BLOCKS,
        (ANY_SPEC, VMEM_SPEC),
        [
            pltpu.VMEM((BLOCKS, bonds, width, width), BF16),
            pltpu.VMEM((pairs, bonds, width, width), BF16),
            pltpu.VMEM((pairs, width, width), BF16),
            pltpu.VMEM((width, pairs, width), BF16),
            pltpu.VMEM((pairs, width, width), BF16),
            pltpu.VMEM((bonds, width, width), BF16),
            pltpu.VMEM((pairs, width, width), F32),
            pltpu.SemaphoreType.DMA((BLOCKS + 2,)),
            pltpu.SemaphoreType.DMA,
            pltpu.SemaphoreType.DMA((pairs,)),
        ],
    )(charge, rank, psi, renv, mpo, x3, *blocks)


def settle(half, other, mine, twin_stat, count):
    width = half.shape[1]
    return call(
        functools.partial(settle_kernel, count),
        "settle",
        10**4,
        (jax.ShapeDtypeStruct((2, width), F32), jax.ShapeDtypeStruct((8, width), F32)),
        [VMEM_SPEC] * 4,
        (VMEM_SPEC, VMEM_SPEC),
        [],
    )(half, other, mine, twin_stat)


def finish(v, out):
    return call(
        finish_kernel,
        "finish",
        10**6,
        jax.ShapeDtypeStruct(v.shape, BF16),
        [ANY_SPEC, VMEM_SPEC],
        ANY_SPEC,
        [
            pltpu.VMEM(v.shape, F32),
            pltpu.VMEM(v.shape, BF16),
            pltpu.SemaphoreType.DMA((FINISH,)),
            pltpu.SemaphoreType.DMA((FINISH,)),
        ],
    )(v, out)


def partner(value, bits):
    axes = ("seg", "sec")
    n = lax.axis_size(axes)
    return lax.ppermute(value, axes, [(i, i ^ bits) for i in range(n)])


def hop(value):
    n = lax.axis_size("sec")
    return lax.ppermute(value, "sec", [(i, (i + (2 if i % 2 == 0 else -2)) % n) for i in range(n)])


def cross_hop(value):
    n = lax.axis_size("sec")
    return lax.ppermute(value, "sec", [(i, (i + (-2 if i % 2 == 0 else 2)) % n ^ 1) for i in range(n)])


def twin(value):
    n = lax.axis_size("sec")
    return lax.ppermute(value, "sec", [(i, i ^ 1) for i in range(n)])


def from_behind(value):
    n = lax.axis_size("seg")
    return lax.ppermute(value, "seg", [(i, i + 1) for i in range(n - 1)])


def shards(psi, env_build, env_right, site_left, site_right, charge, rank):
    nsec = lax.axis_size("sec")
    sector = lax.axis_index("sec")
    segment = lax.axis_index("seg")
    x = psi[0, 0]
    renv = env_right[0, 0]
    pairs, width = x.shape[0], x.shape[2]
    count = float(nsec * pairs * width * width)

    env = env_build[0, 0]
    moved = from_behind(env)
    tall = (site_left.shape[0] * pairs, site_left.shape[1])
    ends = (site_left.transpose(0, 2, 3, 1).reshape(tall), site_right.transpose(0, 2, 3, 1).reshape(tall))
    x3 = front(x, renv, *ends, width // 4)
    moved, x3 = lax.optimization_barrier((moved, x3))
    own = jnp.where(segment == 0, env, moved)

    o1 = hop(own)
    waited, ends = lax.optimization_barrier((own, ends))
    mpo = operators(*ends)
    waited, mpo = lax.optimization_barrier((waited, mpo))
    t1 = cross_hop(waited)
    o2 = hop(o1)
    t2 = hop(t1)
    o3 = hop(o2)
    t3 = hop(t2)
    o4 = hop(o3)
    blocks = [own, twin(own), o1, t1, o2, t2, o3, t3]
    blocks += [o4, twin(o4), twin(t3), twin(o3), twin(t2), twin(o2), twin(t1), twin(o1)]
    v, stat = back(charge, rank, x, renv, mpo, x3, blocks)

    twin_stat = partner(stat, 1)
    total = stat + twin_stat
    for bits in (3, 5):
        total = total + partner(total, bits)
    share, out = settle(total, partner(total, 13), stat, twin_stat, count)
    state = finish(v, out)
    for bits in (1, 3, 4, 12):
        share = share + partner(share, nsec * bits + 1)
        if bits == 1:
            share, state = lax.optimization_barrier((share, state))
    wanted = (iota(share.shape, 0) == sector % 2) & (iota(share.shape, 1) <= segment)
    weight = jnp.sum(jnp.where(wanted, share, 0.0))
    return state[None, None], out[1:2, 0], weight.reshape(1, 1)


def solution(mesh):
    return jax.shard_map(
        shards,
        mesh=mesh,
        in_specs=(
            P("seg", "sec", None, None, None),
            P("seg", "sec", None, None, None),
            P("seg", "sec", None, None, None),
            P(),
            P(),
            P(),
            P("sec"),
        ),
        out_specs=(P("seg", "sec", None, None, None), P("seg"), P("seg", "sec")),
        check_vma=False,
    )
```

```python
import functools

import jax
import jax.numpy as jnp
from jax import lax
from jax.experimental import pallas as pl
from jax.experimental.pallas import tpu as pltpu
from jax.sharding import PartitionSpec as P

F32 = jnp.float32
BF16 = jnp.bfloat16


LOCAL = 4
BLOCKS = 16
CHUNK = 32
FINISH = 4
VMEM_LIMIT = 60 * 2**20
SMALL_LIMIT = 8 * 2**20


def iota(shape, dim):
    return lax.broadcasted_iota(jnp.int32, shape, dim)


def pair_mpo(left_ref, right_ref):
    rows, bonds = left_ref.shape
    pairs = LOCAL * LOCAL
    wide = 256
    over_w = (iota((bonds, wide), 0) == iota((bonds, wide), 1) // pairs).astype(BF16)
    big = jnp.dot(right_ref[...], over_w, preferred_element_type=F32)
    same = (iota((rows, wide), 0) % pairs) == (iota((rows, wide), 1) % pairs)
    big = jnp.where(same, big, 0.0).astype(BF16)
    by_m = (iota((16, rows), 0) == iota((16, rows), 1) // pairs).astype(BF16)
    right = jnp.dot(by_m, big, preferred_element_type=F32).astype(BF16)
    joined = jnp.dot(left_ref[...], right[:bonds], preferred_element_type=F32)
    gap = iota((rows, wide), 0) % LOCAL - (iota((rows, wide), 1) // LOCAL) % LOCAL
    out = jnp.zeros((rows, wide), F32)
    for d in range(1 - LOCAL, LOCAL):
        moved = pltpu.roll(pltpu.roll(joined, d % rows, 0), (-LOCAL * d) % wide, 1)
        out = jnp.where(gap == d, moved, out)
    return out[:, :rows].astype(BF16)


def turn(src_ref, xt_ref):
    for j in range(src_ref.shape[1] // 16):
        xt_ref[j * 16 : (j + 1) * 16] = jnp.swapaxes(src_ref[:, j * 16 : (j + 1) * 16, :], 0, 1)


def spread(xt_ref, renv_ref, mpo, x3_ref, begin=0, done=None):
    states, pairs, width = xt_ref.shape
    bonds = renv_ref.shape[0]
    beside = jnp.concatenate([renv_ref[w] for w in range(bonds)], axis=1)
    for start in range(begin, states, CHUNK):
        xa = xt_ref[start : start + CHUNK].reshape(CHUNK * pairs, width)
        first = jnp.dot(xa, beside, preferred_element_type=F32).astype(BF16)
        for at in range(0, CHUNK, 16):
            rows = []
            for i in range(at, at + 16, 2):
                sides = []
                for a in (i, i + 1):
                    row = first[a * pairs : (a + 1) * pairs]
                    sides.append(jnp.concatenate([row[:, w * width : (w + 1) * width] for w in range(bonds)], axis=0))
                out = jnp.dot(mpo, jnp.concatenate(sides, axis=1), preferred_element_type=F32).astype(BF16)
                rows += [out[:, :width], out[:, width:]]
            for l in range(bonds):
                block = jnp.stack([row[l * pairs : (l + 1) * pairs] for row in rows], axis=0)
                x3_ref[:, l, start + at : start + at + 16, :] = jnp.swapaxes(block, 0, 1)
        if done is not None:
            done(start)


def operators_kernel(left_ref, right_ref, mpo_ref):
    mpo_ref[...] = pair_mpo(left_ref, right_ref)


def front_kernel(psi_any, renv_any, left_ref, right_ref, x3_any, psi_ref, renv_ref, xt_ref, x3_ref, sem_ref, out_sem):
    copies = [
        pltpu.make_async_copy(psi_any.at[:, pl.ds(0, psi_ref.shape[1])], psi_ref, sem_ref.at[0]),
        pltpu.make_async_copy(renv_any, renv_ref, sem_ref.at[1]),
    ]
    for copy in copies:
        copy.start()
    mpo = pair_mpo(left_ref, right_ref)
    for copy in copies:
        copy.wait()
    turn(psi_ref, xt_ref)
    sent = []

    def done(at):
        rows = pl.ds(at, CHUNK)
        sent.append(pltpu.make_async_copy(x3_ref.at[:, :, rows], x3_any.at[:, :, rows], out_sem.at[at // CHUNK]))
        sent[-1].start()

    spread(xt_ref, renv_ref, mpo, x3_ref, 0, done)
    for copy in sent:
        copy.wait()


def contract(lenv_ref, slot, x3_ref, q):
    bonds = lenv_ref.shape[1]
    lhs = jnp.concatenate([lenv_ref[slot, l] for l in range(bonds)], axis=1)
    rhs = jnp.concatenate([x3_ref[q, l] for l in range(bonds)], axis=0)
    return jnp.dot(lhs, rhs, preferred_element_type=F32)


def folded(value):
    return jnp.sum(value.reshape(value.shape[0] // 8, 8, value.shape[1]), axis=0)


def slot_of(charge_ref, q):
    sector = lax.axis_index("sec")
    left = (sector - charge_ref[q]) & 15
    core = sector & 1
    ahead = (sector >> 1) - (left >> 1)
    hops = jnp.where(core == 0, ahead, -ahead) & 7
    return 2 * hops + ((left ^ sector) & 1)


def back_kernel(charge_ref, rank_ref, psi_any, renv_any, mpo_ref, x3_any, *rest):
    blocks = rest[:BLOCKS]
    v_any, stat_ref, lenv_ref, x3_ref, u_ref, xt_ref, psi_ref, renv_ref, v_ref = rest[BLOCKS:-3]
    sem_ref, x3_sem, v_sem = rest[-3:]
    pairs, width = psi_ref.shape[0], psi_ref.shape[2]
    done = x3_any.shape[2]
    first = [
        pltpu.make_async_copy(psi_any, psi_ref, sem_ref.at[BLOCKS]),
        pltpu.make_async_copy(renv_any, renv_ref, sem_ref.at[BLOCKS + 1]),
    ]
    second = [pltpu.make_async_copy(blocks[i], lenv_ref.at[i], sem_ref.at[i]) for i in range(BLOCKS)]
    second.append(pltpu.make_async_copy(x3_any, x3_ref.at[:, :, pl.ds(0, done)], x3_sem))
    for copy in first + second:
        copy.start()
    slots = [slot_of(charge_ref, q) for q in range(pairs)]
    keep = iota((width, width), 1) < rank_ref[0]
    zero = jnp.zeros((8, width), F32)
    for copy in first:
        copy.wait()
    turn(psi_ref, xt_ref)
    spread(xt_ref, renv_ref, mpo_ref[...], x3_ref, done)
    for copy in second:
        copy.wait()
    first_sq = zero
    for q in range(pairs):
        h = contract(lenv_ref, slots[q], x3_ref, q)
        u = jnp.where(keep, psi_ref[q].astype(F32) - 0.5 * h, 0.0)
        u_ref[q] = u.astype(BF16)
        first_sq = first_sq + folded(u * u)
    turn(u_ref, xt_ref)
    spread(xt_ref, renv_ref, mpo_ref[...], x3_ref)
    sq, inner, own = zero, zero, zero
    sent = []
    for q in range(pairs):
        h = contract(lenv_ref, slots[q], x3_ref, q)
        x = u_ref[q].astype(F32)
        v = jnp.where(keep, x - 0.5 * h, 0.0)
        v_ref[q] = v
        sent.append(pltpu.make_async_copy(v_ref.at[q], v_any.at[q], v_sem.at[q]))
        sent[-1].start()
        sq, inner, own = sq + folded(v * v), inner + folded(x * h), own + folded(x * x)
    for i, part in enumerate((first_sq, sq, inner, own)):
        stat_ref[i : i + 1] = jnp.sum(part, axis=0, keepdims=True)
    for copy in sent:
        copy.wait()


def settle_kernel(count, half_ref, other_ref, mine_ref, twin_ref, share_ref, out_ref):
    width = half_ref.shape[1]
    total = jnp.sum(half_ref[...] + other_ref[...], axis=1, keepdims=True)
    first_sq, sq, inner, own = [total[i : i + 1] for i in range(4)]
    one = lax.rsqrt(first_sq / count + 1e-06)
    scale = one * lax.rsqrt(one * one * sq / count + 1e-06)
    out_ref[...] = jnp.where(iota((8, width), 0) == 0, scale, inner / own)
    mine = jnp.sum(mine_ref[1:2], axis=1, keepdims=True)
    twin = jnp.sum(twin_ref[1:2], axis=1, keepdims=True)
    row = iota((2, width), 0)
    here = jnp.where(row == (lax.axis_index("sec") & 1), mine, twin)
    share = jnp.log(float(lax.axis_size("sec")) * here / sq)
    share_ref[...] = jnp.where(iota((2, width), 1) == lax.axis_index("seg"), share, 0.0)


def finish_kernel(v_any, out_ref, state_any, v_ref, state_ref, in_sem, out_sem):
    pairs = v_ref.shape[0]
    part = pairs // FINISH
    loads, stores = [], []
    for i in range(FINISH):
        rows = pl.ds(i * part, part)
        loads.append(pltpu.make_async_copy(v_any.at[rows], v_ref.at[rows], in_sem.at[i]))
        stores.append(pltpu.make_async_copy(state_ref.at[rows], state_any.at[rows], out_sem.at[i]))
        loads[i].start()
    scale = out_ref[0:1, :]
    for i in range(FINISH):
        loads[i].wait()
        for q in range(i * part, (i + 1) * part):
            state_ref[q] = (v_ref[q] * scale).astype(BF16)
        stores[i].start()
    for store in stores:
        store.wait()


VMEM_SPEC = pl.BlockSpec(memory_space=pltpu.VMEM)
SMEM_SPEC = pl.BlockSpec(memory_space=pltpu.SMEM)
ANY_SPEC = pl.BlockSpec(memory_space=pl.ANY)


def call(kernel, name, flops, out_shape, in_specs, out_specs, scratch, limit=SMALL_LIMIT):
    return pl.pallas_call(
        kernel,
        out_shape=out_shape,
        in_specs=in_specs,
        out_specs=out_specs,
        scratch_shapes=scratch,
        compiler_params=pltpu.CompilerParams(vmem_limit_bytes=limit),
        cost_estimate=pl.CostEstimate(flops=flops, bytes_accessed=8 * 10**6, transcendentals=0),
        name=name,
    )


def operators(left, right):
    rows = left.shape[0]
    return call(
        operators_kernel,
        "operators",
        10**8,
        jax.ShapeDtypeStruct((rows, rows), BF16),
        [VMEM_SPEC, VMEM_SPEC],
        VMEM_SPEC,
        [],
    )(left, right)


def front(psi, renv, left, right, states):
    pairs, width = psi.shape[0], psi.shape[2]
    bonds = renv.shape[0]
    return call(
        front_kernel,
        "front",
        5 * 10**8,
        jax.ShapeDtypeStruct((pairs, bonds, states, width), BF16),
        [ANY_SPEC, ANY_SPEC, VMEM_SPEC, VMEM_SPEC],
        ANY_SPEC,
        [
            pltpu.VMEM((pairs, states, width), BF16),
            pltpu.VMEM((bonds, width, width), BF16),
            pltpu.VMEM((states, pairs, width), BF16),
            pltpu.VMEM((pairs, bonds, states, width), BF16),
            pltpu.SemaphoreType.DMA((2,)),
            pltpu.SemaphoreType.DMA((states // CHUNK,)),
        ],
        VMEM_LIMIT,
    )(psi, renv, left, right)


def back(charge, rank, psi, renv, mpo, x3, blocks):
    pairs, width = psi.shape[0], psi.shape[2]
    bonds = renv.shape[0]
    return call(
        back_kernel,
        "back",
        4 * 10**9,
        (jax.ShapeDtypeStruct((pairs, width, width), F32), jax.ShapeDtypeStruct((4, width), F32)),
        [SMEM_SPEC, SMEM_SPEC, ANY_SPEC, ANY_SPEC, VMEM_SPEC, ANY_SPEC] + [ANY_SPEC] * BLOCKS,
        (ANY_SPEC, VMEM_SPEC),
        [
            pltpu.VMEM((BLOCKS, bonds, width, width), BF16),
            pltpu.VMEM((pairs, bonds, width, width), BF16),
            pltpu.VMEM((pairs, width, width), BF16),
            pltpu.VMEM((width, pairs, width), BF16),
            pltpu.VMEM((pairs, width, width), BF16),
            pltpu.VMEM((bonds, width, width), BF16),
            pltpu.VMEM((pairs, width, width), F32),
            pltpu.SemaphoreType.DMA((BLOCKS + 2,)),
            pltpu.SemaphoreType.DMA,
            pltpu.SemaphoreType.DMA((pairs,)),
        ],
        VMEM_LIMIT,
    )(charge, rank, psi, renv, mpo, x3, *blocks)


def settle(half, other, mine, twin_stat, count):
    width = half.shape[1]
    return call(
        functools.partial(settle_kernel, count),
        "settle",
        10**4,
        (jax.ShapeDtypeStruct((2, width), F32), jax.ShapeDtypeStruct((8, width), F32)),
        [VMEM_SPEC] * 4,
        (VMEM_SPEC, VMEM_SPEC),
        [],
    )(half, other, mine, twin_stat)


def finish(v, out):
    return call(
        finish_kernel,
        "finish",
        10**6,
        jax.ShapeDtypeStruct(v.shape, BF16),
        [ANY_SPEC, VMEM_SPEC],
        ANY_SPEC,
        [
            pltpu.VMEM(v.shape, F32),
            pltpu.VMEM(v.shape, BF16),
            pltpu.SemaphoreType.DMA((FINISH,)),
            pltpu.SemaphoreType.DMA((FINISH,)),
        ],
    )(v, out)


def partner(value, bits):
    axes = ("seg", "sec")
    n = lax.axis_size(axes)
    return lax.ppermute(value, axes, [(i, i ^ bits) for i in range(n)])


def hop(value):
    n = lax.axis_size("sec")
    return lax.ppermute(value, "sec", [(i, (i + (2 if i % 2 == 0 else -2)) % n) for i in range(n)])


def cross_hop(value):
    n = lax.axis_size("sec")
    return lax.ppermute(value, "sec", [(i, (i + (-2 if i % 2 == 0 else 2)) % n ^ 1) for i in range(n)])


def twin(value):
    n = lax.axis_size("sec")
    return lax.ppermute(value, "sec", [(i, i ^ 1) for i in range(n)])


def from_behind(value):
    n = lax.axis_size("seg")
    return lax.ppermute(value, "seg", [(i, i + 1) for i in range(n - 1)])


def shards(psi, env_build, env_right, site_left, site_right, charge, rank):
    nsec = lax.axis_size("sec")
    sector = lax.axis_index("sec")
    segment = lax.axis_index("seg")
    x = psi[0, 0]
    renv = env_right[0, 0]
    pairs, width = x.shape[0], x.shape[2]
    count = float(nsec * pairs * width * width)

    env = env_build[0, 0]
    moved = from_behind(env)
    tall = (site_left.shape[0] * pairs, site_left.shape[1])
    ends = (site_left.transpose(0, 2, 3, 1).reshape(tall), site_right.transpose(0, 2, 3, 1).reshape(tall))
    x3 = front(x, renv, *ends, width // 4)
    moved, x3 = lax.optimization_barrier((moved, x3))
    own = jnp.where(segment == 0, env, moved)

    o1 = hop(own)
    waited, ends = lax.optimization_barrier((own, ends))
    mpo = operators(*ends)
    waited, mpo = lax.optimization_barrier((waited, mpo))
    t1 = cross_hop(waited)
    o2 = hop(o1)
    t2 = hop(t1)
    o3 = hop(o2)
    t3 = hop(t2)
    o4 = hop(o3)
    blocks = [own, twin(own), o1, t1, o2, t2, o3, t3]
    blocks += [o4, twin(o4), twin(t3), twin(o3), twin(t2), twin(o2), twin(t1), twin(o1)]
    v, stat = back(charge, rank, x, renv, mpo, x3, blocks)

    twin_stat = partner(stat, 1)
    total = stat + twin_stat
    for bits in (3, 5):
        total = total + partner(total, bits)
    share, out = settle(total, partner(total, 13), stat, twin_stat, count)
    state = finish(v, out)
    for bits in (1, 3, 4, 12):
        share = share + partner(share, nsec * bits + 1)
        if bits == 1:
            share, state = lax.optimization_barrier((share, state))
    wanted = (iota(share.shape, 0) == sector % 2) & (iota(share.shape, 1) <= segment)
    weight = jnp.sum(jnp.where(wanted, share, 0.0))
    return state[None, None], out[1:2, 0], weight.reshape(1, 1)


def solution(mesh):
    return jax.shard_map(
        shards,
        mesh=mesh,
        in_specs=(
            P("seg", "sec", None, None, None),
            P("seg", "sec", None, None, None),
            P("seg", "sec", None, None, None),
            P(),
            P(),
            P(),
            P("sec"),
        ),
        out_specs=(P("seg", "sec", None, None, None), P("seg"), P("seg", "sec")),
        check_vma=False,
    )
```

```python
import functools

import jax
import jax.numpy as jnp
from jax import lax
from jax.experimental import pallas as pl
from jax.experimental.pallas import tpu as pltpu
from jax.sharding import PartitionSpec as P

F32 = jnp.float32
BF16 = jnp.bfloat16


LOCAL = 4
BLOCKS = 16
CHUNK = 32
FINISH = 4
VMEM_LIMIT = 60 * 2**20
SMALL_LIMIT = 8 * 2**20


def iota(shape, dim):
    return lax.broadcasted_iota(jnp.int32, shape, dim)


def pair_mpo(left_ref, right_ref):
    rows, bonds = left_ref.shape
    pairs = LOCAL * LOCAL
    wide = 256
    over_w = (iota((bonds, wide), 0) == iota((bonds, wide), 1) // pairs).astype(BF16)
    big = jnp.dot(right_ref[...], over_w, preferred_element_type=F32)
    same = (iota((rows, wide), 0) % pairs) == (iota((rows, wide), 1) % pairs)
    big = jnp.where(same, big, 0.0).astype(BF16)
    by_m = (iota((16, rows), 0) == iota((16, rows), 1) // pairs).astype(BF16)
    right = jnp.dot(by_m, big, preferred_element_type=F32).astype(BF16)
    joined = jnp.dot(left_ref[...], right[:bonds], preferred_element_type=F32)
    gap = iota((rows, wide), 0) % LOCAL - (iota((rows, wide), 1) // LOCAL) % LOCAL
    out = jnp.zeros((rows, wide), F32)
    for d in range(1 - LOCAL, LOCAL):
        moved = pltpu.roll(pltpu.roll(joined, d % rows, 0), (-LOCAL * d) % wide, 1)
        out = jnp.where(gap == d, moved, out)
    return out[:, :rows].astype(BF16)


def turn(src_ref, xt_ref):
    for j in range(src_ref.shape[1] // 16):
        xt_ref[j * 16 : (j + 1) * 16] = jnp.swapaxes(src_ref[:, j * 16 : (j + 1) * 16, :], 0, 1)


def spread(xt_ref, renv_ref, mpo, x3_ref, chunk, begin=0, done=None):
    states, pairs, width = xt_ref.shape
    bonds = renv_ref.shape[0]
    beside = jnp.concatenate([renv_ref[w] for w in range(bonds)], axis=1)
    for start in range(begin, states, chunk):
        xa = xt_ref[start : start + chunk].reshape(chunk * pairs, width)
        first = jnp.dot(xa, beside, preferred_element_type=F32).astype(BF16)
        for at in range(0, chunk, 16):
            rows = []
            for i in range(at, at + 16, 2):
                sides = []
                for a in (i, i + 1):
                    row = first[a * pairs : (a + 1) * pairs]
                    sides.append(jnp.concatenate([row[:, w * width : (w + 1) * width] for w in range(bonds)], axis=0))
                out = jnp.dot(mpo, jnp.concatenate(sides, axis=1), preferred_element_type=F32).astype(BF16)
                rows += [out[:, :width], out[:, width:]]
            for l in range(bonds):
                block = jnp.stack([row[l * pairs : (l + 1) * pairs] for row in rows], axis=0)
                x3_ref[:, l, start + at : start + at + 16, :] = jnp.swapaxes(block, 0, 1)
        if done is not None:
            done(start)


def operators_kernel(left_ref, right_ref, mpo_ref):
    mpo_ref[...] = pair_mpo(left_ref, right_ref)


def front_kernel(psi_any, renv_any, left_ref, right_ref, x3_any, psi_ref, renv_ref, xt_ref, x3_ref, sem_ref, out_sem):
    copies = [
        pltpu.make_async_copy(psi_any.at[:, pl.ds(0, psi_ref.shape[1])], psi_ref, sem_ref.at[0]),
        pltpu.make_async_copy(renv_any, renv_ref, sem_ref.at[1]),
    ]
    for copy in copies:
        copy.start()
    mpo = pair_mpo(left_ref, right_ref)
    for copy in copies:
        copy.wait()
    turn(psi_ref, xt_ref)
    sent = []

    def done(at):
        rows = pl.ds(at, CHUNK)
        sent.append(pltpu.make_async_copy(x3_ref.at[:, :, rows], x3_any.at[:, :, rows], out_sem.at[at // CHUNK]))
        sent[-1].start()

    spread(xt_ref, renv_ref, mpo, x3_ref, CHUNK, 0, done)
    for copy in sent:
        copy.wait()


def contract(lenv_ref, slot, x3_ref, q):
    bonds = lenv_ref.shape[1]
    lhs = jnp.concatenate([lenv_ref[slot, l] for l in range(bonds)], axis=1)
    rhs = jnp.concatenate([x3_ref[q, l] for l in range(bonds)], axis=0)
    return jnp.dot(lhs, rhs, preferred_element_type=F32)


def folded(value):
    return jnp.sum(value.reshape(value.shape[0] // 8, 8, value.shape[1]), axis=0)


def slot_of(charge_ref, q):
    sector = lax.axis_index("sec")
    left = (sector - charge_ref[q]) & 15
    core = sector & 1
    ahead = (sector >> 1) - (left >> 1)
    hops = jnp.where(core == 0, ahead, -ahead) & 7
    return 2 * hops + ((left ^ sector) & 1)


def back_kernel(charge_ref, rank_ref, psi_any, renv_any, mpo_ref, x3_any, *rest):
    blocks = rest[:BLOCKS]
    v_any, stat_ref, lenv_ref, x3_ref, u_ref, xt_ref, psi_ref, renv_ref, v_ref = rest[BLOCKS:-3]
    sem_ref, x3_sem, v_sem = rest[-3:]
    pairs, width = psi_ref.shape[0], psi_ref.shape[2]
    done = x3_any.shape[2]
    first = [
        pltpu.make_async_copy(psi_any, psi_ref, sem_ref.at[BLOCKS]),
        pltpu.make_async_copy(renv_any, renv_ref, sem_ref.at[BLOCKS + 1]),
    ]
    second = [pltpu.make_async_copy(blocks[i], lenv_ref.at[i], sem_ref.at[i]) for i in range(BLOCKS)]
    second.append(pltpu.make_async_copy(x3_any, x3_ref.at[:, :, pl.ds(0, done)], x3_sem))
    for copy in first + second:
        copy.start()
    slots = [slot_of(charge_ref, q) for q in range(pairs)]
    keep = iota((width, width), 1) < rank_ref[0]
    zero = jnp.zeros((8, width), F32)
    for copy in first:
        copy.wait()
    turn(psi_ref, xt_ref)
    spread(xt_ref, renv_ref, mpo_ref[...], x3_ref, CHUNK, done)
    for copy in second:
        copy.wait()
    first_sq = zero
    for q in range(pairs):
        h = contract(lenv_ref, slots[q], x3_ref, q)
        u = jnp.where(keep, psi_ref[q].astype(F32) - 0.5 * h, 0.0)
        u_ref[q] = u.astype(BF16)
        first_sq = first_sq + folded(u * u)
    turn(u_ref, xt_ref)
    spread(xt_ref, renv_ref, mpo_ref[...], x3_ref, CHUNK)
    sq, inner, own = zero, zero, zero
    sent = []
    for q in range(pairs):
        h = contract(lenv_ref, slots[q], x3_ref, q)
        x = u_ref[q].astype(F32)
        v = jnp.where(keep, x - 0.5 * h, 0.0)
        v_ref[q] = v
        sent.append(pltpu.make_async_copy(v_ref.at[q], v_any.at[q], v_sem.at[q]))
        sent[-1].start()
        sq, inner, own = sq + folded(v * v), inner + folded(x * h), own + folded(x * x)
    for i, part in enumerate((first_sq, sq, inner, own)):
        stat_ref[i : i + 1] = jnp.sum(part, axis=0, keepdims=True)
    for copy in sent:
        copy.wait()


def settle_kernel(count, half_ref, other_ref, pair_ref, share_ref, out_ref):
    width = half_ref.shape[1]
    total = jnp.sum(half_ref[...] + other_ref[...], axis=1, keepdims=True)
    first_sq, sq, inner, own = [total[i : i + 1] for i in range(4)]
    one = lax.rsqrt(first_sq / count + 1e-06)
    scale = one * lax.rsqrt(one * one * sq / count + 1e-06)
    out_ref[...] = jnp.where(iota((8, width), 0) == 0, scale, inner / own)
    mine = jnp.sum(pair_ref[0:1], axis=1, keepdims=True)
    twin = jnp.sum(pair_ref[1:2], axis=1, keepdims=True)
    row = iota((2, width), 0)
    here = jnp.where(row == (lax.axis_index("sec") & 1), mine, twin)
    share = jnp.log(float(lax.axis_size("sec")) * here / sq)
    share_ref[...] = jnp.where(iota((2, width), 1) == lax.axis_index("seg"), share, 0.0)


def finish_kernel(v_any, out_ref, state_any, v_ref, state_ref, in_sem, out_sem):
    pairs = v_ref.shape[0]
    part = pairs // FINISH
    loads, stores = [], []
    for i in range(FINISH):
        rows = pl.ds(i * part, part)
        loads.append(pltpu.make_async_copy(v_any.at[rows], v_ref.at[rows], in_sem.at[i]))
        stores.append(pltpu.make_async_copy(state_ref.at[rows], state_any.at[rows], out_sem.at[i]))
        loads[i].start()
    scale = out_ref[0:1, :]
    for i in range(FINISH):
        loads[i].wait()
        for q in range(i * part, (i + 1) * part):
            state_ref[q] = (v_ref[q] * scale).astype(BF16)
        stores[i].start()
    for store in stores:
        store.wait()


VMEM_SPEC = pl.BlockSpec(memory_space=pltpu.VMEM)
SMEM_SPEC = pl.BlockSpec(memory_space=pltpu.SMEM)
ANY_SPEC = pl.BlockSpec(memory_space=pl.ANY)


def call(kernel, name, flops, out_shape, in_specs, out_specs, scratch, limit=SMALL_LIMIT):
    return pl.pallas_call(
        kernel,
        out_shape=out_shape,
        in_specs=in_specs,
        out_specs=out_specs,
        scratch_shapes=scratch,
        compiler_params=pltpu.CompilerParams(vmem_limit_bytes=limit),
        cost_estimate=pl.CostEstimate(flops=flops, bytes_accessed=8 * 10**6, transcendentals=0),
        name=name,
    )


def operators(left, right):
    rows = left.shape[0]
    return call(
        operators_kernel,
        "operators",
        10**8,
        jax.ShapeDtypeStruct((rows, rows), BF16),
        [VMEM_SPEC, VMEM_SPEC],
        VMEM_SPEC,
        [],
    )(left, right)


def front(psi, renv, left, right, states):
    pairs, width = psi.shape[0], psi.shape[2]
    bonds = renv.shape[0]
    return call(
        front_kernel,
        "front",
        5 * 10**8,
        jax.ShapeDtypeStruct((pairs, bonds, states, width), BF16),
        [ANY_SPEC, ANY_SPEC, VMEM_SPEC, VMEM_SPEC],
        ANY_SPEC,
        [
            pltpu.VMEM((pairs, states, width), BF16),
            pltpu.VMEM((bonds, width, width), BF16),
            pltpu.VMEM((states, pairs, width), BF16),
            pltpu.VMEM((pairs, bonds, states, width), BF16),
            pltpu.SemaphoreType.DMA((2,)),
            pltpu.SemaphoreType.DMA((states // CHUNK,)),
        ],
        VMEM_LIMIT,
    )(psi, renv, left, right)


def back(charge, rank, psi, renv, mpo, x3, blocks):
    pairs, width = psi.shape[0], psi.shape[2]
    bonds = renv.shape[0]
    return call(
        back_kernel,
        "back",
        4 * 10**9,
        (jax.ShapeDtypeStruct((pairs, width, width), F32), jax.ShapeDtypeStruct((4, width), F32)),
        [SMEM_SPEC, SMEM_SPEC, ANY_SPEC, ANY_SPEC, VMEM_SPEC, ANY_SPEC] + [ANY_SPEC] * BLOCKS,
        (ANY_SPEC, VMEM_SPEC),
        [
            pltpu.VMEM((BLOCKS, bonds, width, width), BF16),
            pltpu.VMEM((pairs, bonds, width, width), BF16),
            pltpu.VMEM((pairs, width, width), BF16),
            pltpu.VMEM((width, pairs, width), BF16),
            pltpu.VMEM((pairs, width, width), BF16),
            pltpu.VMEM((bonds, width, width), BF16),
            pltpu.VMEM((pairs, width, width), F32),
            pltpu.SemaphoreType.DMA((BLOCKS + 2,)),
            pltpu.SemaphoreType.DMA,
            pltpu.SemaphoreType.DMA((pairs,)),
        ],
        VMEM_LIMIT,
    )(charge, rank, psi, renv, mpo, x3, *blocks)


def settle(half, other, pair, count):
    width = half.shape[1]
    return call(
        functools.partial(settle_kernel, count),
        "settle",
        10**4,
        (jax.ShapeDtypeStruct((2, width), F32), jax.ShapeDtypeStruct((8, width), F32)),
        [VMEM_SPEC] * 3,
        (VMEM_SPEC, VMEM_SPEC),
        [],
    )(half, other, pair)


def finish(v, out):
    return call(
        finish_kernel,
        "finish",
        10**6,
        jax.ShapeDtypeStruct(v.shape, BF16),
        [ANY_SPEC, VMEM_SPEC],
        ANY_SPEC,
        [
            pltpu.VMEM(v.shape, F32),
            pltpu.VMEM(v.shape, BF16),
            pltpu.SemaphoreType.DMA((FINISH,)),
            pltpu.SemaphoreType.DMA((FINISH,)),
        ],
    )(v, out)


def partner(value, bits):
    axes = ("seg", "sec")
    n = lax.axis_size(axes)
    return lax.ppermute(value, axes, [(i, i ^ bits) for i in range(n)])


def hop(value):
    n = lax.axis_size("sec")
    return lax.ppermute(value, "sec", [(i, (i + (2 if i % 2 == 0 else -2)) % n) for i in range(n)])


def cross_hop(value):
    n = lax.axis_size("sec")
    return lax.ppermute(value, "sec", [(i, (i + (-2 if i % 2 == 0 else 2)) % n ^ 1) for i in range(n)])


def twin(value):
    n = lax.axis_size("sec")
    return lax.ppermute(value, "sec", [(i, i ^ 1) for i in range(n)])


def from_behind(value):
    n = lax.axis_size("seg")
    return lax.ppermute(value, "seg", [(i, i + 1) for i in range(n - 1)])


def shards(psi, env_build, env_right, site_left, site_right, charge, rank):
    nsec = lax.axis_size("sec")
    sector = lax.axis_index("sec")
    segment = lax.axis_index("seg")
    x = psi[0, 0]
    renv = env_right[0, 0]
    pairs, width = x.shape[0], x.shape[2]
    count = float(nsec * pairs * width * width)

    env = env_build[0, 0]
    moved = from_behind(env)
    tall = (site_left.shape[0] * pairs, site_left.shape[1])
    ends = (site_left.transpose(0, 2, 3, 1).reshape(tall), site_right.transpose(0, 2, 3, 1).reshape(tall))
    x3 = front(x, renv, *ends, width // 4)
    moved, x3 = lax.optimization_barrier((moved, x3))
    own = jnp.where(segment == 0, env, moved)

    o1 = hop(own)
    waited, ends = lax.optimization_barrier((own, ends))
    mpo = operators(*ends)
    waited, mpo = lax.optimization_barrier((waited, mpo))
    t1 = cross_hop(waited)
    o2 = hop(o1)
    t2 = hop(t1)
    o3 = hop(o2)
    t3 = hop(t2)
    o4 = hop(o3)
    blocks = [own, twin(own), o1, t1, o2, t2, o3, t3]
    blocks += [o4, twin(o4), twin(t3), twin(o3), twin(t2), twin(o2), twin(t1), twin(o1)]
    v, stat = back(charge, rank, x, renv, mpo, x3, blocks)

    twin_stat = partner(stat, 1)
    total = stat + twin_stat
    pair = jnp.concatenate([stat[1:2], twin_stat[1:2]], axis=0)
    got, pair = lax.optimization_barrier((partner(total, 3), pair))
    total = total + got
    total = total + partner(total, 5)
    share, out = settle(total, partner(total, 13), pair, count)
    state = finish(v, out)
    for bits in (1, 3, 4, 12):
        share = share + partner(share, nsec * bits + 1)
        if bits == 3:
            share, state = lax.optimization_barrier((share, state))
    wanted = (iota(share.shape, 0) == sector % 2) & (iota(share.shape, 1) <= segment)
    weight = jnp.sum(jnp.where(wanted, share, 0.0))
    return state[None, None], out[1:2, 0], weight.reshape(1, 1)


def solution(mesh):
    return jax.shard_map(
        shards,
        mesh=mesh,
        in_specs=(
            P("seg", "sec", None, None, None),
            P("seg", "sec", None, None, None),
            P("seg", "sec", None, None, None),
            P(),
            P(),
            P(),
            P("sec"),
        ),
        out_specs=(P("seg", "sec", None, None, None), P("seg"), P("seg", "sec")),
        check_vma=False,
    )
```
